128 devices in a mesh: harm: 8 (over x, z_hi), rows: 16 (over y, z_lo, core).
Axes of the slice: x: 4, y: 4, z: 4 (z_hi: 2, z_lo: 2; z = z_hi * 2 + z_lo), core: 2. Of those that a mesh axis runs over, the one named last changes fastest.
Arguments:
- pressure: float32 [24, 1024, 2, 1024], P('harm', 'rows'), may hold values from -6 to 6
- contrast: float32 [1024, 1024], P('rows'), may hold values from -0.02 to 0.02
- absorption: float32 [1024, 1024], P('rows'), may hold values from 1e-05 to 0.0001
- nonlinearity: float32 [1024, 1024], P('rows'), may hold values from 0.5 to 2
Outputs:
- pressure_out: float32 [24, 1024, 2, 1024], P('harm', 'rows')
The draws below stay inside these ranges and needn't reach their ends.
All inputs are finite; a program needn't handle non-finite values.
Results may differ from the reference program's by a relative error of at most 0.0003.
Values sent between devices are 32-bit elements; how exact they have to be, the bound alone decides.
No kernel may reach another device: no remote copies, remote signals or barrier semaphores. Data moves between devices by JAX's collectives and lax.ppermute only.
A program may use at most 128 MiB of HBM per device.

```python
import math
import jax
import jax.numpy as jnp
from jax import lax

H = 24
N = 1024
PLANES = 2
DZ = 128


def block_scale(key, dims, pieces, least, largest):
    def one(dim, blocks):
        draws = jax.random.uniform(jax.random.fold_in(jax.random.fold_in(key, 6), dim), (blocks,), jnp.float32, least / len(pieces), largest / len(pieces))
        return jnp.repeat(jnp.exp(draws), dims[dim] // blocks).reshape((-1,) + (1,) * (len(dims) - dim - 1))

    loudness = one(*pieces[0])
    for cut in pieces[1:]:
        loudness = loudness * one(*cut)
    return loudness


def normal_values(key, shape, deviation, most, split=(), kind=jnp.bfloat16):
    array = jax.random.normal(key, shape, jnp.float32) * deviation
    if len(split) > 0:
        array = block_scale(key, shape, split, -0.22, 0.18) * array
    return jnp.clip(array, min=-most, max=most).astype(kind)


def setup_inputs(seed: int = 0) -> dict:
    keys = jax.random.split(jax.random.key(seed), 5)
    pressure = normal_values(keys[0], (H, N, 2, N), 1.0, 6.0, ((0, 8), (1, 16)), jnp.float32)
    contrast = jnp.clip(jax.random.uniform(keys[1], (N, N), jnp.float32, -0.02, 0.02) * block_scale(keys[1], (N, N), ((0, 16),), -0.4, 0.0), -0.02, 0.02)
    absorption = jnp.clip(jnp.exp(math.log(0.0001) - 2.3025851 * jax.random.uniform(keys[2], (N, N), jnp.float32) ** block_scale(keys[2], (N, N), ((0, 16),), -0.2, 0.2)), 9.999999747378752e-06, 0.0001)
    nonlinearity = jnp.clip(jnp.exp(math.log(2.0) - 1.3862944 * jax.random.uniform(keys[3], (N, N), jnp.float32) ** block_scale(keys[3], (N, N), ((0, 16),), -0.2, 0.2)), 0.5, 2.0)
    return {"pressure": pressure, "contrast": contrast, "absorption": absorption, "nonlinearity": nonlinearity}


def squared_freq_at(indices, length):
    centred = jnp.where(indices < length // 2, indices, indices - length).astype(jnp.float32)
    scaled = centred * (2.0 * math.pi / length)
    return scaled * scaled

def propagator(wave_number, down_square, across_square, march_step):
    axial_square = wave_number * wave_number - down_square - across_square
    axial_root = jnp.sqrt(jnp.abs(axial_square))
    phase_turn = march_step * axial_root
    propagating = axial_square >= 0.0
    prop_real = jnp.where(propagating, jnp.cos(phase_turn), jnp.exp(-phase_turn))
    prop_imag = jnp.where(propagating, jnp.sin(phase_turn), 0.0)
    return (prop_real, prop_imag)

def screen_pair(real_part, imag_part, orders, contrast, absorption, march_step, harmonic_count):
    damping = jnp.exp(-absorption[None] * jnp.power(orders, 1.1) * march_step)
    angle = 3.0 / harmonic_count * orders * march_step * contrast[None]
    factor_real = damping * jnp.cos(angle)
    factor_imag = damping * jnp.sin(angle)
    return (real_part * factor_real - imag_part * factor_imag, real_part * factor_imag + imag_part * factor_real)

def couple(real_part, imag_part, gain):
    harmonic_count = real_part.shape[0]
    coupled_real = []
    coupled_imag = []
    for harmonic in range(1, harmonic_count + 1):
        source_real = jnp.zeros_like(real_part[0])
        source_imag = jnp.zeros_like(real_part[0])
        if harmonic > 1:
            first_real = real_part[:harmonic - 1]
            first_imag = imag_part[:harmonic - 1]
            second_real = real_part[harmonic - 2::-1]
            second_imag = imag_part[harmonic - 2::-1]
            source_real = source_real + lax.optimization_barrier(jnp.sum(first_real * second_real - first_imag * second_imag, axis=0))
            source_imag = source_imag + lax.optimization_barrier(jnp.sum(first_real * second_imag + first_imag * second_real, axis=0))
        if harmonic < harmonic_count:
            high_real = real_part[harmonic:]
            high_imag = imag_part[harmonic:]
            low_real = real_part[:harmonic_count - harmonic]
            low_imag = imag_part[:harmonic_count - harmonic]
            source_real = source_real + 2.0 * lax.optimization_barrier(jnp.sum(high_real * low_real + high_imag * low_imag, axis=0))
            source_imag = source_imag + 2.0 * lax.optimization_barrier(jnp.sum(high_imag * low_real - high_real * low_imag, axis=0))
        weight = harmonic * gain
        coupled_real.append(real_part[harmonic - 1] - weight * source_imag)
        coupled_imag.append(imag_part[harmonic - 1] + weight * source_real)
    return (jnp.stack(coupled_real, axis=0), jnp.stack(coupled_imag, axis=0))

def reference(pressure, contrast, absorption, nonlinearity):
    march_step = float(DZ)
    orders = jnp.arange(1, H + 1, dtype=jnp.int32).astype(jnp.float32)
    wave_numbers = orders * (3.0 / H)
    spatial_square = squared_freq_at(jnp.arange(N, dtype=jnp.int32), N)
    prop_real, prop_imag = propagator(wave_numbers[:, None, None], spatial_square[None, :, None], spatial_square[None, None, :], march_step)
    real_part = pressure[:, :, 0, :]
    imag_part = pressure[:, :, 1, :]
    gain = nonlinearity * (1.0 / (H * math.sqrt(H)))
    for plane_index in range(PLANES):
        spectrum = jnp.fft.fft2(real_part + 1j * imag_part, axes=(1, 2))
        spectrum = spectrum * (prop_real + 1j * prop_imag)
        marched = jnp.fft.ifft2(spectrum, axes=(1, 2))
        real_part, imag_part = screen_pair(jnp.real(marched), jnp.imag(marched), orders[:, None, None], contrast, absorption, march_step, H)
        real_part, imag_part = couple(real_part, imag_part, gain)
    return jnp.stack([real_part, imag_part], axis=2)
```

```python
import functools
import math

import jax
import jax.numpy as jnp
import ml_dtypes
import numpy as np
from jax import lax
from jax.experimental import pallas as pl
from jax.experimental.pallas import tpu as pltpu
from jax.sharding import PartitionSpec as P

H = 24
N = 1024
PLANES = 2
DZ = 128
RADIX = 8
SUB = N // RADIX
HALF = SUB // 2
ROOT_HALF = math.sqrt(0.5)
VMEM_LIMIT = 56 * 1024 * 1024


def split_constant(table):
    high = table.astype(np.float32).astype(ml_dtypes.bfloat16)
    low = (table - high.astype(np.float64)).astype(np.float32).astype(ml_dtypes.bfloat16)
    return high, low


def sub_angles():
    index = np.arange(SUB)
    return 2.0 * np.pi / SUB * ((index[:, None] * index[None, :]) % SUB)


def lane_matrices():
    cosine, sine = np.cos(sub_angles()), np.sin(sub_angles())
    forward_real = np.concatenate([cosine, sine], 0)
    forward_imag = np.concatenate([-sine, cosine], 0)
    inverse_real = np.concatenate([cosine, -sine], 0)
    inverse_imag = np.concatenate([sine, cosine], 0)
    forward = np.concatenate(
        [
            forward_real[:, :HALF],
            forward_imag[:, :HALF],
            forward_real[:, HALF:],
            forward_imag[:, HALF:],
        ],
        1,
    )
    inverse = np.concatenate([inverse_real, inverse_imag], 1)
    inverse = np.concatenate(
        [
            inverse[:HALF],
            inverse[SUB : SUB + HALF],
            inverse[HALF:SUB],
            inverse[SUB + HALF :],
        ],
        0,
    )
    return split_constant(forward), split_constant(inverse)


def lane_twiddles():
    angle = 2.0 * np.pi / N * (np.arange(RADIX)[:, None] * np.arange(SUB)[None, :])
    return np.cos(angle).astype(np.float32), np.sin(angle).astype(np.float32)


def row_matrices():
    both = np.concatenate([np.cos(sub_angles()), np.sin(sub_angles())], 0)
    high, low = split_constant(both)
    return np.concatenate([high, high], 1), low


def row_twiddles():
    angle = 2.0 * np.pi / N * (np.arange(RADIX)[:, None] * np.arange(SUB)[None, :])
    sign = np.where(np.arange(SUB) < HALF, 1.0, -1.0)
    cosine = np.broadcast_to(np.cos(angle)[:, :, None], (RADIX, SUB, SUB))
    sine = np.sin(angle)[:, :, None] * sign[None, None, :]
    return cosine.astype(np.float32), sine.astype(np.float32)


def split_value(value):
    high = value.astype(jnp.bfloat16)
    low = (value - high.astype(jnp.float32)).astype(jnp.bfloat16)
    return high, low


def add(left, right):
    return tuple(a + b for a, b in zip(left, right))


def subtract(left, right):
    return tuple(a - b for a, b in zip(left, right))


def scale(value, factor):
    return tuple(a * factor for a in value)


def turn_pair(direction):
    def turn(value):
        real, imag = value
        return (imag, -real) if direction < 0 else (-imag, real)

    return turn


def butterflies(points, turn):
    even = [add(points[k], points[k + 4]) for k in range(4)]
    odd = [subtract(points[k], points[k + 4]) for k in range(4)]
    turned = turn(odd[1])
    first = scale(add(odd[1], turned), ROOT_HALF)
    second = turn(odd[2])
    turned = turn(odd[3])
    third = scale(subtract(turned, odd[3]), ROOT_HALF)
    out = [None] * RADIX
    for offset, (a, b, c, d) in ((0, even), (1, (odd[0], first, second, third))):
        sum_ac, diff_ac = add(a, c), subtract(a, c)
        sum_bd, diff_bd = add(b, d), turn(subtract(b, d))
        out[offset] = add(sum_ac, sum_bd)
        out[offset + 4] = subtract(sum_ac, sum_bd)
        out[offset + 2] = add(diff_ac, diff_bd)
        out[offset + 6] = subtract(diff_ac, diff_bd)
    return out


def triple_dot(high, low, matrix_high, matrix_low):
    def product(left, right):
        return jnp.dot(left, right, preferred_element_type=jnp.float32)

    return product(high, matrix_high) + (product(low, matrix_high) + product(high, matrix_low))


def twiddle_pair(value, cosine, sine, direction):
    real, imag = value
    if direction < 0:
        return real * cosine + imag * sine, imag * cosine - real * sine
    return real * cosine - imag * sine, imag * cosine + real * sine


def forward_lanes(points, store, cosine_ref, sine_ref):
    for m, value in enumerate(butterflies(points, turn_pair(-1))):
        if m > 0:
            value = twiddle_pair(value, cosine_ref[m : m + 1], sine_ref[m : m + 1], -1)
        store(m, *split_value(jnp.concatenate(value, axis=1)))


def first_kernel(
    in_ref, gh_ref, gl_ref, cosine_ref, sine_ref, out_ref, high_ref, low_ref
):
    rows = out_ref.shape[2]
    for start in range(0, rows, 16):
        points = [
            tuple(
                in_ref[pl.ds(start * 16 + 2 * k + c, 16, stride=16), :] for c in range(2)
            )
            for k in range(RADIX)
        ]

        def store(m, high, low):
            high_ref[m, start : start + 16, :] = high
            low_ref[m, start : start + 16, :] = low

        forward_lanes(points, store, cosine_ref, sine_ref)
    for m in range(RADIX):
        result = triple_dot(high_ref[m], low_ref[m], gh_ref[...], gl_ref[...])
        out_ref[2 * m, 0] = result[:, :SUB]
        out_ref[2 * m + 1, 0] = result[:, SUB:]


def whole(shape):
    return pl.BlockSpec(shape, lambda *index: (0,) * len(shape))


def first_transform(pressure, constants):
    local_harm, rows = pressure.shape[0], pressure.shape[1]
    lines = pressure.reshape(local_harm, rows, 2, RADIX, SUB).transpose(0, 1, 3, 2, 4)
    lines = lines.reshape(local_harm * rows * 16, SUB)
    (gh, gl), _, (cosine, sine) = constants["lane"]
    return pl.pallas_call(
        first_kernel,
        grid=(local_harm,),
        in_specs=[
            pl.BlockSpec((rows * 16, SUB), lambda n: (n, 0)),
            whole(gh.shape),
            whole(gl.shape),
            whole(cosine.shape),
            whole(sine.shape),
        ],
        out_specs=pl.BlockSpec((16, 1, rows, SUB), lambda n: (0, n, 0, 0)),
        out_shape=jax.ShapeDtypeStruct((16, local_harm, rows, SUB), jnp.float32),
        scratch_shapes=[
            pltpu.VMEM((RADIX, rows, 2 * SUB), jnp.bfloat16),
            pltpu.VMEM((RADIX, rows, 2 * SUB), jnp.bfloat16),
        ],
        compiler_params=pltpu.CompilerParams(vmem_limit_bytes=VMEM_LIMIT),
        cost_estimate=pl.CostEstimate(
            flops=3 * 2 * local_harm * rows * RADIX * 65536,
            bytes_accessed=2 * lines.size * 4,
            transcendentals=0,
        ),
        name="first_transform",
    )(lines, gh, gl, cosine, sine)


def march_kernel(
    load, in_ref, pr_ref, pi_ref, mh_ref, ml_ref, cosine_ref, sine_ref, out_ref, part_ref, spec_ref
):
    lane = lax.broadcasted_iota(jnp.int32, (8, SUB), 1)
    sign = jnp.where(lane < HALF, 1.0, -1.0).astype(jnp.float32)

    def swap(value):
        return pltpu.roll(value, HALF, 1)

    def turn_forward(value):
        return (sign * swap(value[0]),)

    def turn_inverse(value):
        return (-sign * swap(value[0]),)

    def rows_product():
        halves = part_ref[...]
        return jnp.dot(
            mh_ref[...], halves, preferred_element_type=jnp.float32
        ) + jnp.dot(ml_ref[...], halves[:SUB], preferred_element_type=jnp.float32)

    for pair in range(SUB // 16):
        outs = []
        for tile in (2 * pair, 2 * pair + 1):
            points = [(load(in_ref, 2 * k + tile // 8, tile % 8),) for k in range(RADIX)]
            values = butterflies(points, turn_forward)
            rows = slice(8 * tile, 8 * tile + 8)
            outs.append(
                [
                    value[0]
                    if m == 0
                    else value[0] * cosine_ref[m, rows] + swap(value[0]) * sine_ref[m, rows]
                    for m, value in enumerate(values)
                ]
            )
        for m in range(RADIX):
            high, low = split_value(jnp.concatenate([outs[0][m], outs[1][m]], 0))
            part_ref[16 * pair : 16 * pair + 16, SUB * m : SUB * m + SUB] = high
            part_ref[SUB + 16 * pair : SUB + 16 * pair + 16, SUB * m : SUB * m + SUB] = low
    spec_ref[...] = rows_product()
    for m in range(RADIX):
        lanes = slice(SUB * m, SUB * m + SUB)
        for pair in range(SUB // 16):
            outs = []
            for tile in (2 * pair, 2 * pair + 1):
                rows = slice(8 * tile, 8 * tile + 8)
                value = spec_ref[rows, lanes] + sign * swap(
                    spec_ref[SUB + 8 * tile : SUB + 8 * tile + 8, lanes]
                )
                outs.append(value * pr_ref[0, m, rows] + swap(value) * pi_ref[0, m, rows])
            high, low = split_value(jnp.concatenate(outs, 0))
            part_ref[16 * pair : 16 * pair + 16, lanes] = high
            part_ref[SUB + 16 * pair : SUB + 16 * pair + 16, lanes] = low
    spec_ref[...] = rows_product()
    for tile in range(SUB // 8):
        rows = slice(8 * tile, 8 * tile + 8)
        points = []
        for m in range(RADIX):
            lanes = slice(SUB * m, SUB * m + SUB)
            value = spec_ref[rows, lanes] - sign * swap(
                spec_ref[SUB + 8 * tile : SUB + 8 * tile + 8, lanes]
            )
            if m > 0:
                value = value * cosine_ref[m, rows] - swap(value) * sine_ref[m, rows]
            points.append((value,))
        for k, value in enumerate(butterflies(points, turn_inverse)):
            out_ref[tile % 8, 2 * k + tile // 8, 0] = value[0]


def march(wavefield, prop_real, prop_imag, constants, by_rows):
    harm_count, row_count = 8, 16
    if by_rows:
        local_harm = wavefield.shape[1]
        in_spec = pl.BlockSpec((16, 1, 64, SUB), lambda n: (0, n, 0, 0))

        def load(ref, block, tile):
            return ref[block, 0, 8 * tile : 8 * tile + 8, :]
    else:
        local_harm = wavefield.shape[2]
        in_spec = pl.BlockSpec((harm_count, row_count, 1, 8, SUB), lambda n: (0, 0, n, 0, 0))

        def load(ref, block, tile):
            return ref[tile, block, 0]

    mh, ml = constants["row_matrices"]
    cosine, sine = constants["row_twiddles"]
    prop_spec = pl.BlockSpec((1, RADIX, SUB, SUB), lambda n: (n, 0, 0, 0))
    return pl.pallas_call(
        functools.partial(march_kernel, load),
        grid=(local_harm,),
        in_specs=[
            in_spec,
            prop_spec,
            prop_spec,
            whole(mh.shape),
            whole(ml.shape),
            whole(cosine.shape),
            whole(sine.shape),
        ],
        out_specs=pl.BlockSpec(
            (harm_count, row_count, 1, 8, SUB), lambda n: (0, 0, n, 0, 0)
        ),
        out_shape=jax.ShapeDtypeStruct(
            (harm_count, row_count, local_harm, 8, SUB), jnp.float32
        ),
        scratch_shapes=[
            pltpu.VMEM((2 * SUB, N), jnp.bfloat16),
            pltpu.VMEM((2 * SUB, N), jnp.float32),
        ],
        compiler_params=pltpu.CompilerParams(vmem_limit_bytes=VMEM_LIMIT),
        cost_estimate=pl.CostEstimate(
            flops=2 * 2 * 2 * local_harm * 256 * 256 * N,
            bytes_accessed=4 * wavefield.size * 4,
            transcendentals=0,
        ),
        name="march",
    )(wavefield, prop_real, prop_imag, mh, ml, cosine, sine)


def pair_order():
    block = 4
    order = []
    for low in range(0, H, block):
        for high in range(low, H, block):
            order += [
                (m, l)
                for m in range(high + 1, high + block + 1)
                for l in range(low + 1, low + block + 1)
                if m > l
            ]
    return order


def couple_pixels(load, gain, store):
    total_real = [None] * (H + 1)
    total_imag = [None] * (H + 1)

    def accumulate(n, real, imag):
        total_real[n] = real if total_real[n] is None else total_real[n] + real
        total_imag[n] = imag if total_imag[n] is None else total_imag[n] + imag

    for m, l in pair_order():
        (a, b), (c, d) = load(m), load(l)
        ac, bd, ad, bc = a * c, b * d, a * d, b * c
        accumulate(m - l, ac + bd, bc - ad)
        if m + l <= H:
            accumulate(m + l, ac - bd, ad + bc)
    for m in range(1, H // 2 + 1):
        a, b = load(m)
        accumulate(2 * m, 0.5 * (a * a - b * b), a * b)
    for n in range(1, H + 1):
        a, b = load(n)
        weight = (2.0 * n) * gain
        if total_real[n] is None:
            store(n, a, b)
        else:
            store(n, a - weight * total_imag[n], b + weight * total_real[n])


def pixel_kernel(
    last,
    in_ref,
    fr_ref,
    fi_ref,
    gain_ref,
    gh_ref,
    gl_ref,
    ih_ref,
    il_ref,
    cosine_ref,
    sine_ref,
    out_ref,
    high_ref,
    low_ref,
    line_ref,
    field_ref,
):
    local_harm = H // 8

    def tile_of(n, r):
        return in_ref[n // local_harm, r, n % local_harm]

    for n in range(0, H, 2):
        for m in range(RADIX):
            value = jnp.concatenate(
                [
                    jnp.concatenate([tile_of(n + i, 2 * m), tile_of(n + i, 2 * m + 1)], 1)
                    for i in range(2)
                ],
                0,
            )
            high, low = split_value(value)
            high_ref[m, 8 * n : 8 * n + 16, :] = high
            low_ref[m, 8 * n : 8 * n + 16, :] = low
    for m in range(RADIX):
        line_ref[m] = triple_dot(high_ref[m], low_ref[m], ih_ref[...], il_ref[...])
    for n in range(H):
        rows = slice(8 * n, 8 * n + 8)
        points = []
        for m in range(RADIX):
            value = (line_ref[m, rows, :SUB], line_ref[m, rows, SUB:])
            if m > 0:
                value = twiddle_pair(value, cosine_ref[m : m + 1], sine_ref[m : m + 1], 1)
            points.append(value)
        for k, (real, imag) in enumerate(butterflies(points, turn_pair(1))):
            lanes = slice(SUB * k, SUB * k + SUB)
            factor_real, factor_imag = fr_ref[n, :, lanes], fi_ref[n, :, lanes]
            field_ref[k, 2 * n] = real * factor_real - imag * factor_imag
            field_ref[k, 2 * n + 1] = real * factor_imag + imag * factor_real

    def one_block(k, carry):
        def load(n):
            return field_ref[k, 2 * n - 2], field_ref[k, 2 * n - 1]

        def store(n, real, imag):
            if last:
                start = 128 * (n - 1) + 2 * k
                out_ref[pl.ds(start, 8, stride=16), :] = real
                out_ref[pl.ds(start + 1, 8, stride=16), :] = imag
            else:
                line_ref[k, 8 * n - 8 : 8 * n, :SUB] = real
                line_ref[k, 8 * n - 8 : 8 * n, SUB:] = imag

        couple_pixels(load, gain_ref[k], store)
        return carry

    lax.fori_loop(0, RADIX, one_block, 0)
    if last:
        return
    for n in range(0, H, 2):
        rows = slice(8 * n, 8 * n + 16)
        points = [(line_ref[k, rows, :SUB], line_ref[k, rows, SUB:]) for k in range(RADIX)]

        def store_parts(m, high, low):
            high_ref[m, rows, :] = high
            low_ref[m, rows, :] = low

        forward_lanes(points, store_parts, cosine_ref, sine_ref)
    for m in range(RADIX):
        result = triple_dot(high_ref[m], low_ref[m], gh_ref[...], gl_ref[...])
        for n in range(H):
            for half in range(2):
                out_ref[n // local_harm, 2 * m + half, n % local_harm] = result[
                    8 * n : 8 * n + 8, SUB * half : SUB * half + SUB
                ]


def pixels(wavefield, factor_real, factor_imag, gain, constants, last):
    (gh, gl), (ih, il), (cosine, sine) = constants["lane"]
    operands = [wavefield, factor_real, factor_imag, gain, gh, gl, ih, il, cosine, sine]
    out_shape = (H * 8 * 16, SUB) if last else wavefield.shape
    return pl.pallas_call(
        functools.partial(pixel_kernel, last),
        in_specs=[pl.BlockSpec(memory_space=pltpu.VMEM) for _ in operands],
        out_specs=pl.BlockSpec(memory_space=pltpu.VMEM),
        out_shape=jax.ShapeDtypeStruct(out_shape, jnp.float32),
        scratch_shapes=[
            pltpu.VMEM((RADIX, 8 * H, 2 * SUB), jnp.bfloat16),
            pltpu.VMEM((RADIX, 8 * H, 2 * SUB), jnp.bfloat16),
            pltpu.VMEM((RADIX, 8 * H, 2 * SUB), jnp.float32),
            pltpu.VMEM((RADIX, 2 * H, 8, SUB), jnp.float32),
        ],
        compiler_params=pltpu.CompilerParams(vmem_limit_bytes=VMEM_LIMIT),
        cost_estimate=pl.CostEstimate(
            flops=2 * 3 * 2 * 8 * H * RADIX * 65536,
            bytes_accessed=4 * wavefield.size * 4,
            transcendentals=0,
        ),
        name="pixels_last" if last else "pixels",
    )(*operands)


def squared_freq_at(indices, length):
    centred = jnp.where(indices < length // 2, indices, indices - length).astype(jnp.float32)
    scaled = centred * (2.0 * math.pi / length)
    return scaled * scaled


def propagator(wave_number, down_square, across_square, march_step):
    axial_square = wave_number * wave_number - down_square - across_square
    axial_root = jnp.sqrt(jnp.abs(axial_square))
    phase_turn = march_step * axial_root
    propagating = axial_square >= 0.0
    prop_real = jnp.where(propagating, jnp.cos(phase_turn), jnp.exp(-phase_turn))
    prop_imag = jnp.where(propagating, jnp.sin(phase_turn), 0.0)
    return (prop_real, prop_imag)


def propagator_tables(local_harm):
    orders = (
        lax.axis_index("harm") * local_harm + jnp.arange(local_harm, dtype=jnp.int32) + 1
    ).astype(jnp.float32)
    place = lax.axis_index("rows")
    down = RADIX * jnp.arange(SUB, dtype=jnp.int32)[None, :] + jnp.arange(
        RADIX, dtype=jnp.int32
    )[:, None]
    lane = jnp.arange(SUB, dtype=jnp.int32)
    across = RADIX * (lax.rem(place, 2) * HALF + lax.rem(lane, HALF)) + place // 2
    real, imag = propagator(
        (3.0 / H * orders)[:, None, None, None],
        squared_freq_at(down, N)[None, :, :, None],
        squared_freq_at(across, N)[None, None, None, :],
        float(DZ),
    )
    factor = 1.0 / (N * N)
    sign = jnp.where(lane < HALF, -factor, factor).astype(jnp.float32)
    return real * factor, imag * sign


def screen_tables(contrast, absorption):
    orders = jnp.arange(1, H + 1, dtype=jnp.int32).astype(jnp.float32)[:, None, None]
    damping = jnp.exp(-absorption[None] * jnp.power(orders, 1.1) * float(DZ))
    angle = 3.0 / H * orders * float(DZ) * contrast[None]
    return damping * jnp.cos(angle), damping * jnp.sin(angle)


def shards(pressure, contrast, absorption, nonlinearity):
    local_harm = pressure.shape[0]
    constants = {
        "lane": lane_matrices() + (lane_twiddles(),),
        "row_matrices": row_matrices(),
        "row_twiddles": row_twiddles(),
    }
    constants = jax.tree.map(jnp.asarray, constants)
    axes = ("harm", "rows")
    pixel_rows = 8
    row_start = lax.axis_index("harm") * pixel_rows

    def own_rows(values):
        return lax.dynamic_slice_in_dim(values, row_start, pixel_rows, 0)

    gain = own_rows(nonlinearity) * (1.0 / (H * math.sqrt(H)))
    gain = gain.reshape(pixel_rows, RADIX, SUB).transpose(1, 0, 2)
    prop_real, prop_imag = propagator_tables(local_harm)
    factor_real, factor_imag = screen_tables(own_rows(contrast), own_rows(absorption))

    lines = first_transform(pressure, constants)
    lines = lax.all_to_all(lines, "rows", 0, 0, tiled=True)
    for plane_index in range(PLANES):
        marched = march(lines, prop_real, prop_imag, constants, plane_index == 0)
        shape = marched.shape
        marched = lax.all_to_all(marched.reshape((128,) + shape[2:]), axes, 0, 0, tiled=True)
        last = plane_index == PLANES - 1
        lines = pixels(
            marched.reshape(shape), factor_real, factor_imag, gain, constants, last
        )
        if not last:
            lines = lax.all_to_all(lines.reshape((128,) + shape[2:]), axes, 0, 0, tiled=True)
            lines = lines.reshape(shape)
    out = lines.reshape(8, local_harm * pixel_rows * 16, SUB)
    out = lax.all_to_all(out, "harm", 0, 0, tiled=True)
    out = out.reshape(8, local_harm, pixel_rows, RADIX, 2, SUB)
    out = out.transpose(1, 0, 2, 4, 3, 5)
    return out.reshape(local_harm, 8 * pixel_rows, 2, N)


def solution(mesh):
    in_specs = (P("harm", "rows", None, None), P("rows", None), P("rows", None), P("rows", None))
    out_specs = P("harm", "rows", None, None)
    return jax.shard_map(shards, mesh=mesh, in_specs=in_specs, out_specs=out_specs, check_vma=False)
```

```python
import functools
import math

import jax
import jax.numpy as jnp
import ml_dtypes
import numpy as np
from jax import lax
from jax.experimental import pallas as pl
from jax.experimental.pallas import tpu as pltpu
from jax.sharding import PartitionSpec as P

H = 24
N = 1024
PLANES = 2
DZ = 128
RADIX = 8
SUB = N // RADIX
HALF = SUB // 2
ROOT_HALF = math.sqrt(0.5)
VMEM_LIMIT = 20 * 1024 * 1024


def split_constant(table):
    high = table.astype(np.float32).astype(ml_dtypes.bfloat16)
    low = (table - high.astype(np.float64)).astype(np.float32).astype(ml_dtypes.bfloat16)
    return high, low


def stack_constant(table):
    high, low = split_constant(table)
    return np.concatenate([high, high, low], 0)


def sub_angles():
    index = np.arange(SUB)
    return 2.0 * np.pi / SUB * ((index[:, None] * index[None, :]) % SUB)


def lane_matrices():
    cosine, sine = np.cos(sub_angles()), np.sin(sub_angles())
    forward_real = np.concatenate([cosine, sine], 0)
    forward_imag = np.concatenate([-sine, cosine], 0)
    inverse_real = np.concatenate([cosine, -sine], 0)
    inverse_imag = np.concatenate([sine, cosine], 0)
    forward = np.concatenate(
        [
            forward_real[:, :HALF],
            forward_imag[:, :HALF],
            forward_real[:, HALF:],
            forward_imag[:, HALF:],
        ],
        1,
    )
    inverse = np.concatenate([inverse_real, inverse_imag], 1)
    inverse = np.concatenate(
        [
            inverse[:HALF],
            inverse[SUB : SUB + HALF],
            inverse[HALF:SUB],
            inverse[SUB + HALF :],
        ],
        0,
    )
    return stack_constant(forward), stack_constant(inverse)


def lane_twiddles():
    angle = 2.0 * np.pi / N * (np.arange(RADIX)[:, None] * np.arange(SUB)[None, :])
    return np.stack([np.cos(angle), np.sin(angle)]).astype(np.float32)


def row_matrices():
    both = np.concatenate([np.cos(sub_angles()), np.sin(sub_angles())], 0)
    high, low = split_constant(both)
    return np.concatenate([high, high, low], 1)


def row_twiddles():
    angle = 2.0 * np.pi / N * (np.arange(RADIX)[:, None] * np.arange(SUB)[None, :])
    sign = np.where(np.arange(SUB) < HALF, 1.0, -1.0)
    cosine = np.broadcast_to(np.cos(angle)[:, :, None], (RADIX, SUB, SUB))
    sine = np.sin(angle)[:, :, None] * sign[None, None, :]
    return np.stack([cosine, sine]).astype(np.float32)


def split_value(value):
    high = value.astype(jnp.bfloat16)
    low = (value - high.astype(jnp.float32)).astype(jnp.bfloat16)
    return high, low


def add(left, right):
    return tuple(a + b for a, b in zip(left, right))


def subtract(left, right):
    return tuple(a - b for a, b in zip(left, right))


def scale(value, factor):
    return tuple(a * factor for a in value)


def turn_pair(direction):
    def turn(value):
        real, imag = value
        return (imag, -real) if direction < 0 else (-imag, real)

    return turn


def butterflies(points, turn):
    even = [add(points[k], points[k + 4]) for k in range(4)]
    odd = [subtract(points[k], points[k + 4]) for k in range(4)]
    turned = turn(odd[1])
    first = scale(add(odd[1], turned), ROOT_HALF)
    second = turn(odd[2])
    turned = turn(odd[3])
    third = scale(subtract(turned, odd[3]), ROOT_HALF)
    out = [None] * RADIX
    for offset, (a, b, c, d) in ((0, even), (1, (odd[0], first, second, third))):
        sum_ac, diff_ac = add(a, c), subtract(a, c)
        sum_bd, diff_bd = add(b, d), turn(subtract(b, d))
        out[offset] = add(sum_ac, sum_bd)
        out[offset + 4] = subtract(sum_ac, sum_bd)
        out[offset + 2] = add(diff_ac, diff_bd)
        out[offset + 6] = subtract(diff_ac, diff_bd)
    return out


def product(left, right):
    return jnp.dot(left, right, preferred_element_type=jnp.float32)


def store_parts(part_ref, rows, value):
    high, low = split_value(value)
    part_ref[rows, :256] = high
    part_ref[rows, 256:512] = low
    part_ref[rows, 512:] = high


def twiddle_pair(value, cosine, sine, direction):
    real, imag = value
    if direction < 0:
        return real * cosine + imag * sine, imag * cosine - real * sine
    return real * cosine - imag * sine, imag * cosine + real * sine


def fetch(sources, targets, sems):
    copies = [
        pltpu.make_async_copy(source, target, sems.at[index])
        for index, (source, target) in enumerate(zip(sources, targets))
    ]
    for copy in copies:
        copy.start()
    return copies


def forward_lanes(points, store, twiddle_ref):
    for m, value in enumerate(butterflies(points, turn_pair(-1))):
        if m > 0:
            value = twiddle_pair(value, twiddle_ref[0, m : m + 1], twiddle_ref[1, m : m + 1], -1)
        store(m, jnp.concatenate(value, axis=1))


def first_kernel(
    in_ref, g_hbm, twiddle_hbm, out_ref, line_ref, part_ref, g_ref, twiddle_ref, sems
):
    local_harm, rows = out_ref.shape[1], out_ref.shape[2]
    lines = rows * 2 * RADIX
    copies = fetch(
        [in_ref.at[pl.ds(n * lines, lines)] for n in range(local_harm)] + [twiddle_hbm, g_hbm],
        [line_ref.at[n] for n in range(local_harm)] + [twiddle_ref, g_ref],
        sems,
    )
    copies[local_harm].wait()
    for n in range(local_harm):
        copies[n].wait()

        def one_tile(t, carry, n=n):
            start = pl.multiple_of(t * 16, 16)
            points = [
                tuple(
                    line_ref[n, pl.ds(start * 16 + 2 * k + c, 16, stride=16), :]
                    for c in range(2)
                )
                for k in range(RADIX)
            ]

            def store(m, value):
                first = (m * local_harm + n) * rows
                store_parts(part_ref, pl.ds(pl.multiple_of(first + start, 16), 16), value)

            forward_lanes(points, store, twiddle_ref)
            return carry

        lax.fori_loop(0, rows // 16, one_tile, 0)
    copies[local_harm + 1].wait()
    result = product(part_ref[...], g_ref[...])
    for m in range(RADIX):
        for n in range(local_harm):
            first = (m * local_harm + n) * rows
            out_ref[2 * m, n] = result[first : first + rows, :SUB]
            out_ref[2 * m + 1, n] = result[first : first + rows, SUB:]


IN_VMEM = pl.BlockSpec(memory_space=pltpu.VMEM)
IN_HBM = pl.BlockSpec(memory_space=pltpu.HBM)


def in_vmem(*arrays):
    return [pltpu.with_memory_space_constraint(array, pltpu.VMEM) for array in arrays]


def in_hbm(*arrays):
    return [pltpu.with_memory_space_constraint(array, pltpu.HBM) for array in arrays]


def first_transform(pressure, constants):
    local_harm, rows = pressure.shape[0], pressure.shape[1]
    lines = pressure.reshape(local_harm, rows, 2, RADIX, SUB).transpose(0, 1, 3, 2, 4)
    lines = lines.reshape(local_harm * rows * 16, SUB)
    forward, _, twiddles = constants["lane"]
    return pl.pallas_call(
        first_kernel,
        in_specs=[IN_HBM] * 3,
        out_specs=IN_VMEM,
        out_shape=pltpu.VMEM((16, local_harm, rows, SUB), jnp.float32),
        scratch_shapes=[
            pltpu.VMEM((local_harm, rows * 16, SUB), jnp.float32),
            pltpu.VMEM((RADIX * local_harm * rows, 768), jnp.bfloat16),
            pltpu.VMEM(forward.shape, forward.dtype),
            pltpu.VMEM(twiddles.shape, twiddles.dtype),
            pltpu.SemaphoreType.DMA((local_harm + 2,)),
        ],
        compiler_params=pltpu.CompilerParams(vmem_limit_bytes=VMEM_LIMIT),
        cost_estimate=pl.CostEstimate(
            flops=3 * 2 * local_harm * rows * RADIX * 65536,
            bytes_accessed=2 * lines.size * 4,
            transcendentals=0,
        ),
        name="first_transform",
    )(*in_hbm(lines, forward, twiddles))


def march_fetching(
    in_ref,
    prop_hbm,
    m_hbm,
    twiddle_hbm,
    screen_ref,
    gain_ref,
    out_ref,
    part_ref,
    spec_ref,
    prop_ref,
    m_ref,
    twiddle_ref,
    sems,
):
    local_harm = out_ref.shape[2]
    copies = fetch(
        [twiddle_hbm, m_hbm] + [prop_hbm.at[:, n] for n in range(local_harm)],
        [twiddle_ref, m_ref] + [prop_ref.at[:, n] for n in range(local_harm)],
        sems,
    )
    copies[0].wait()
    copies[1].wait()

    def wait(n):
        pltpu.make_async_copy(prop_hbm.at[:, n], prop_ref.at[:, n], sems.at[2 + n]).wait()

    march_kernel(
        True, wait, in_ref, prop_ref, m_ref, twiddle_ref, out_ref, part_ref, spec_ref
    )


def march_kernel(
    by_rows, wait, in_ref, prop_ref, m_ref, twiddle_ref, out_ref, part_ref, spec_ref
):
    local_harm = out_ref.shape[2]
    lane = lax.broadcasted_iota(jnp.int32, (8, SUB), 1)
    sign = jnp.where(lane < HALF, 1.0, -1.0).astype(jnp.float32)

    def swap(value):
        return pltpu.roll(value, HALF, 1)

    def turn_forward(value):
        return (sign * swap(value[0]),)

    def turn_inverse(value):
        return (-sign * swap(value[0]),)

    def load(n, block, tile):
        if by_rows:
            return in_ref[block, n, 8 * tile : 8 * tile + 8, :]
        return in_ref[tile, block, n]

    def store(pair, m, value):
        lanes = slice(SUB * m, SUB * m + SUB)
        high, low = split_value(value)
        for part, data in enumerate((high, low, high)):
            first = SUB * part + 16 * pair
            part_ref[first : first + 16, lanes] = data

    def one_harmonic(n, carry):
        for pair in range(SUB // 16):
            outs = []
            for tile in (2 * pair, 2 * pair + 1):
                points = [(load(n, 2 * k + tile // 8, tile % 8),) for k in range(RADIX)]
                values = butterflies(points, turn_forward)
                rows = slice(8 * tile, 8 * tile + 8)
                outs.append(
                    [
                        value[0]
                        if m == 0
                        else value[0] * twiddle_ref[0, m, rows]
                        + swap(value[0]) * twiddle_ref[1, m, rows]
                        for m, value in enumerate(values)
                    ]
                )
            for m in range(RADIX):
                store(pair, m, jnp.concatenate([outs[0][m], outs[1][m]], 0))
        spec_ref[...] = product(m_ref[...], part_ref[...])
        wait(n)
        for m in range(RADIX):
            lanes = slice(SUB * m, SUB * m + SUB)
            for pair in range(SUB // 16):
                outs = []
                for tile in (2 * pair, 2 * pair + 1):
                    rows = slice(8 * tile, 8 * tile + 8)
                    value = spec_ref[rows, lanes] + sign * swap(
                        spec_ref[SUB + 8 * tile : SUB + 8 * tile + 8, lanes]
                    )
                    outs.append(value * prop_ref[0, n, m, rows] + swap(value) * prop_ref[1, n, m, rows])
                store(pair, m, jnp.concatenate(outs, 0))
        spec_ref[...] = product(m_ref[...], part_ref[...])
        for tile in range(SUB // 8):
            rows = slice(8 * tile, 8 * tile + 8)
            points = []
            for m in range(RADIX):
                lanes = slice(SUB * m, SUB * m + SUB)
                value = spec_ref[rows, lanes] - sign * swap(
                    spec_ref[SUB + 8 * tile : SUB + 8 * tile + 8, lanes]
                )
                if m > 0:
                    value = (
                        value * twiddle_ref[0, m, rows] - swap(value) * twiddle_ref[1, m, rows]
                    )
                points.append((value,))
            for k, value in enumerate(butterflies(points, turn_inverse)):
                out_ref[tile % 8, 2 * k + tile // 8, n] = value[0]
        return carry

    lax.fori_loop(0, local_harm, one_harmonic, 0)


def march(wavefield, prop, after, constants, by_rows):
    local_harm = wavefield.shape[1 if by_rows else 2]
    tables = [prop, constants["row_matrices"], constants["row_twiddles"]]
    scratch = [
        pltpu.VMEM((3 * SUB, N), jnp.bfloat16),
        pltpu.VMEM((2 * SUB, N), jnp.float32),
    ]
    if by_rows:
        kernel = march_fetching
        operands = in_vmem(wavefield) + in_hbm(*tables, *after)
        in_specs = [IN_VMEM] + [IN_HBM] * (len(operands) - 1)
        scratch += [pltpu.VMEM(table.shape, table.dtype) for table in tables]
        scratch.append(pltpu.SemaphoreType.DMA((2 + local_harm,)))
    else:
        kernel = functools.partial(march_kernel, False, lambda n: None)
        operands = in_vmem(wavefield, *tables)
        in_specs = [IN_VMEM] * len(operands)
    return pl.pallas_call(
        kernel,
        in_specs=in_specs,
        out_specs=IN_VMEM,
        out_shape=pltpu.VMEM((8, 16, local_harm, 8, SUB), jnp.float32),
        scratch_shapes=scratch,
        compiler_params=pltpu.CompilerParams(vmem_limit_bytes=VMEM_LIMIT),
        cost_estimate=pl.CostEstimate(
            flops=2 * 2 * 2 * local_harm * 256 * 256 * N,
            bytes_accessed=4 * wavefield.size * 4,
            transcendentals=0,
        ),
        name="march",
    )(*operands)


def pair_order():
    block = 4
    order = []
    for low in range(0, H, block):
        for high in range(low, H, block):
            order += [
                (m, l)
                for m in range(high + 1, high + block + 1)
                for l in range(low + 1, low + block + 1)
                if m > l
            ]
    return order


def couple_pixels(load, gain, store):
    total_real = [None] * (H + 1)
    total_imag = [None] * (H + 1)

    def accumulate(n, real, imag):
        total_real[n] = real if total_real[n] is None else total_real[n] + real
        total_imag[n] = imag if total_imag[n] is None else total_imag[n] + imag

    for m, l in pair_order():
        (a, b), (c, d) = load(m), load(l)
        ac, bd, ad, bc = a * c, b * d, a * d, b * c
        accumulate(m - l, ac + bd, bc - ad)
        if m + l <= H:
            accumulate(m + l, ac - bd, ad + bc)
    for m in range(1, H // 2 + 1):
        a, b = load(m)
        accumulate(2 * m, 0.5 * (a * a - b * b), a * b)
    for n in range(1, H + 1):
        a, b = load(n)
        weight = (2.0 * n) * gain
        if total_real[n] is None:
            store(n, a, b)
        else:
            store(n, a - weight * total_imag[n], b + weight * total_real[n])


def pixel_kernel(
    last,
    in_ref,
    inverse_ref,
    twiddle_ref,
    screen_ref,
    gain_ref,
    forward_ref,
    out_ref,
    part_ref,
    line_ref,
    field_ref,
):
    local_harm = H // 8
    height = 8 * H

    def tile_of(n, r):
        return in_ref[n // local_harm, r, n % local_harm]

    for n in range(0, H, 2):
        for m in range(RADIX):
            value = jnp.concatenate(
                [
                    jnp.concatenate([tile_of(n + i, 2 * m), tile_of(n + i, 2 * m + 1)], 1)
                    for i in range(2)
                ],
                0,
            )
            first = height * m + 8 * n
            store_parts(part_ref, slice(first, first + 16), value)
    line_ref[...] = product(part_ref[...], inverse_ref[...])

    def one_order(n, carry):
        points = []
        for m in range(RADIX):
            rows = pl.ds(pl.multiple_of(height * m + 8 * n, 8), 8)
            value = (line_ref[rows, :SUB], line_ref[rows, SUB:])
            if m > 0:
                value = twiddle_pair(value, twiddle_ref[0, m : m + 1], twiddle_ref[1, m : m + 1], 1)
            points.append(value)
        for k, (real, imag) in enumerate(butterflies(points, turn_pair(1))):
            lanes = slice(SUB * k, SUB * k + SUB)
            factor_real, factor_imag = screen_ref[0, n, :, lanes], screen_ref[1, n, :, lanes]
            field_ref[k, 2 * n] = real * factor_real - imag * factor_imag
            field_ref[k, 2 * n + 1] = real * factor_imag + imag * factor_real
        return carry

    lax.fori_loop(0, H, one_order, 0, unroll=2)

    def one_block(k, carry):
        def load(n):
            return field_ref[k, 2 * n - 2], field_ref[k, 2 * n - 1]

        def store(n, real, imag):
            if last:
                start = 128 * (n - 1) + 2 * k
                out_ref[pl.ds(start, 8, stride=16), :] = real
                out_ref[pl.ds(start + 1, 8, stride=16), :] = imag
            else:
                rows = pl.ds(pl.multiple_of(height * k + 8 * n - 8, 8), 8)
                line_ref[rows, :SUB] = real
                line_ref[rows, SUB:] = imag

        couple_pixels(load, gain_ref[k], store)
        return carry

    lax.fori_loop(0, RADIX, one_block, 0)
    if last:
        return

    def one_pair(pair, carry):
        def rows(block):
            return pl.ds(pl.multiple_of(height * block + 16 * pair, 16), 16)

        points = [(line_ref[rows(k), :SUB], line_ref[rows(k), SUB:]) for k in range(RADIX)]
        forward_lanes(
            points,
            lambda m, value: store_parts(part_ref, rows(m), value),
            twiddle_ref,
        )
        return carry

    lax.fori_loop(0, H // 2, one_pair, 0)
    result = product(part_ref[...], forward_ref[...])
    for m in range(RADIX):
        for n in range(H):
            first = height * m + 8 * n
            for half in range(2):
                out_ref[n // local_harm, 2 * m + half, n % local_harm] = result[
                    first : first + 8, SUB * half : SUB * half + SUB
                ]


def pixels(wavefield, screen, gain, constants, last):
    forward, inverse, twiddles = constants["lane"]
    tables = [inverse, twiddles, screen, gain, forward]
    operands = in_vmem(wavefield, *tables)
    out_shape = (H * 8 * 16, SUB) if last else wavefield.shape
    return pl.pallas_call(
        functools.partial(pixel_kernel, last),
        in_specs=[IN_VMEM] * len(operands),
        out_specs=IN_VMEM,
        out_shape=pltpu.VMEM(out_shape, jnp.float32),
        scratch_shapes=[
            pltpu.VMEM((RADIX * 8 * H, 768), jnp.bfloat16),
            pltpu.VMEM((RADIX * 8 * H, 2 * SUB), jnp.float32),
            pltpu.VMEM((RADIX, 2 * H, 8, SUB), jnp.float32),
        ],
        compiler_params=pltpu.CompilerParams(vmem_limit_bytes=VMEM_LIMIT),
        cost_estimate=pl.CostEstimate(
            flops=2 * 3 * 2 * 8 * H * RADIX * 65536,
            bytes_accessed=4 * wavefield.size * 4,
            transcendentals=0,
        ),
        name="pixels_last" if last else "pixels",
    )(*operands)


def order_kernel(in_ref, out_ref, sems):
    groups, local_harm = in_ref.shape[:2]
    pairs = [(h, n) for h in range(groups) for n in range(local_harm)]
    copies = fetch(
        [in_ref.at[h, n] for h, n in pairs], [out_ref.at[n, h] for h, n in pairs], sems
    )
    for copy in copies:
        copy.wait()


def order_rows(blocks):
    groups, local_harm = blocks.shape[:2]
    return pl.pallas_call(
        order_kernel,
        in_specs=[IN_VMEM],
        out_specs=IN_HBM,
        out_shape=jax.ShapeDtypeStruct((local_harm, groups) + blocks.shape[2:], blocks.dtype),
        scratch_shapes=[pltpu.SemaphoreType.DMA((groups * local_harm,))],
        name="order_rows",
    )(*in_vmem(blocks))


def squared_freq_at(indices, length):
    centred = jnp.where(indices < length // 2, indices, indices - length).astype(jnp.float32)
    scaled = centred * (2.0 * math.pi / length)
    return scaled * scaled


def propagator(wave_number, down_square, across_square, march_step):
    axial_square = wave_number * wave_number - down_square - across_square
    axial_root = jnp.sqrt(jnp.abs(axial_square))
    phase_turn = march_step * axial_root
    propagating = axial_square >= 0.0
    prop_real = jnp.where(propagating, jnp.cos(phase_turn), jnp.exp(-phase_turn))
    prop_imag = jnp.where(propagating, jnp.sin(phase_turn), 0.0)
    return (prop_real, prop_imag)


def propagator_tables(local_harm):
    orders = (
        lax.axis_index("harm") * local_harm + jnp.arange(local_harm, dtype=jnp.int32) + 1
    ).astype(jnp.float32)
    place = lax.axis_index("rows")
    down = RADIX * jnp.arange(SUB, dtype=jnp.int32)[None, :] + jnp.arange(
        RADIX, dtype=jnp.int32
    )[:, None]
    lane = jnp.arange(SUB, dtype=jnp.int32)
    across = RADIX * (lax.rem(place, 2) * HALF + lax.rem(lane, HALF)) + place // 2
    real, imag = propagator(
        (3.0 / H * orders)[:, None, None, None],
        squared_freq_at(down, N)[None, :, :, None],
        squared_freq_at(across, N)[None, None, None, :],
        float(DZ),
    )
    factor = 1.0 / (N * N)
    sign = jnp.where(lane < HALF, -factor, factor).astype(jnp.float32)
    return jnp.stack([real * factor, imag * sign])


def screen_tables(contrast, absorption):
    orders = jnp.arange(1, H + 1, dtype=jnp.int32).astype(jnp.float32)[:, None, None]
    damping = jnp.exp(-absorption[None] * jnp.power(orders, 1.1) * float(DZ))
    angle = 3.0 / H * orders * float(DZ) * contrast[None]
    return jnp.stack([damping * jnp.cos(angle), damping * jnp.sin(angle)])


def shards(pressure, contrast, absorption, nonlinearity):
    local_harm = pressure.shape[0]
    constants = {
        "lane": lane_matrices() + (lane_twiddles(),),
        "row_matrices": row_matrices(),
        "row_twiddles": row_twiddles(),
    }
    constants = jax.tree.map(jnp.asarray, constants)
    axes = ("harm", "rows")
    pixel_rows = 8
    row_start = lax.axis_index("harm") * pixel_rows

    def own_rows(values):
        return lax.dynamic_slice_in_dim(values, row_start, pixel_rows, 0)

    gain = own_rows(nonlinearity) * (1.0 / (H * math.sqrt(H)))
    gain = gain.reshape(pixel_rows, RADIX, SUB).transpose(1, 0, 2)
    prop = propagator_tables(local_harm)
    screen = screen_tables(own_rows(contrast), own_rows(absorption))

    lines = first_transform(pressure, constants)
    lines = lax.all_to_all(lines, "rows", 0, 0, tiled=True)
    for plane_index in range(PLANES):
        marched = march(lines, prop, (screen, gain), constants, plane_index == 0)
        shape = marched.shape
        marched = lax.all_to_all(marched.reshape((128,) + shape[2:]), axes, 0, 0, tiled=True)
        last = plane_index == PLANES - 1
        lines = pixels(marched.reshape(shape), screen, gain, constants, last)
        if not last:
            lines = lax.all_to_all(lines.reshape((128,) + shape[2:]), axes, 0, 0, tiled=True)
            lines = lines.reshape(shape)
    out = lines.reshape(8, local_harm, pixel_rows * 16, SUB)
    out = lax.all_to_all(out, "harm", 0, 0, tiled=True)
    out = order_rows(out).reshape(local_harm, 8 * pixel_rows, RADIX, 2, SUB)
    return out.transpose(0, 1, 3, 2, 4).reshape(local_harm, 8 * pixel_rows, 2, N)


def solution(mesh):
    in_specs = (P("harm", "rows", None, None), P("rows", None), P("rows", None), P("rows", None))
    out_specs = P("harm", "rows", None, None)
    return jax.shard_map(shards, mesh=mesh, in_specs=in_specs, out_specs=out_specs, check_vma=False)
```

```python
import functools
import math

import jax
import jax.numpy as jnp
import ml_dtypes
import numpy as np
from jax import lax
from jax.experimental import pallas as pl
from jax.experimental.pallas import tpu as pltpu
from jax.sharding import PartitionSpec as P

H = 24
N = 1024
PLANES = 2
DZ = 128
RADIX = 8
SUB = N // RADIX
HALF = SUB // 2
ROOT_HALF = math.sqrt(0.5)
VMEM_LIMIT = 20 * 1024 * 1024


def split_constant(table):
    high = table.astype(np.float32).astype(ml_dtypes.bfloat16)
    low = (table - high.astype(np.float64)).astype(np.float32).astype(ml_dtypes.bfloat16)
    return high, low


def stack_constant(table):
    high, low = split_constant(table)
    return np.concatenate([high, high, low], 0)


def sub_angles():
    index = np.arange(SUB)
    return 2.0 * np.pi / SUB * ((index[:, None] * index[None, :]) % SUB)


def lane_matrices():
    cosine, sine = np.cos(sub_angles()), np.sin(sub_angles())
    forward = np.block([[cosine, -sine], [sine, cosine]])
    inverse = np.block([[cosine, sine], [-sine, cosine]])
    order = np.arange(2 * SUB).reshape(2, 2, HALF).transpose(1, 0, 2).reshape(-1)
    tables = (forward, inverse, forward[:, order], inverse[order])
    return tuple(stack_constant(table) for table in tables)


def lane_twiddles():
    angle = 2.0 * np.pi / N * (np.arange(RADIX)[:, None] * np.arange(SUB)[None, :])
    return np.stack([np.cos(angle), np.sin(angle)]).astype(np.float32)


def split_value(value):
    high = value.astype(jnp.bfloat16)
    low = (value - high.astype(jnp.float32)).astype(jnp.bfloat16)
    return high, low


def add(left, right):
    return tuple(a + b for a, b in zip(left, right))


def subtract(left, right):
    return tuple(a - b for a, b in zip(left, right))


def scale(value, factor):
    return tuple(a * factor for a in value)


def turn_pair(direction):
    def turn(value):
        real, imag = value
        return (imag, -real) if direction < 0 else (-imag, real)

    return turn


def butterflies(points, turn):
    even = [add(points[k], points[k + 4]) for k in range(4)]
    odd = [subtract(points[k], points[k + 4]) for k in range(4)]
    turned = turn(odd[1])
    first = scale(add(odd[1], turned), ROOT_HALF)
    second = turn(odd[2])
    turned = turn(odd[3])
    third = scale(subtract(turned, odd[3]), ROOT_HALF)
    out = [None] * RADIX
    for offset, (a, b, c, d) in ((0, even), (1, (odd[0], first, second, third))):
        sum_ac, diff_ac = add(a, c), subtract(a, c)
        sum_bd, diff_bd = add(b, d), turn(subtract(b, d))
        out[offset] = add(sum_ac, sum_bd)
        out[offset + 4] = subtract(sum_ac, sum_bd)
        out[offset + 2] = add(diff_ac, diff_bd)
        out[offset + 6] = subtract(diff_ac, diff_bd)
    return out


def product(left, right):
    return jnp.dot(left, right, preferred_element_type=jnp.float32)


def store_parts(part_ref, rows, value):
    high, low = split_value(value)
    part_ref[rows, :256] = high
    part_ref[rows, 256:512] = low
    part_ref[rows, 512:] = high


def twiddle_pair(value, cosine, sine, direction):
    real, imag = value
    if direction < 0:
        return real * cosine + imag * sine, imag * cosine - real * sine
    return real * cosine - imag * sine, imag * cosine + real * sine


def fetch(sources, targets, sems):
    copies = [
        pltpu.make_async_copy(source, target, sems.at[index])
        for index, (source, target) in enumerate(zip(sources, targets))
    ]
    for copy in copies:
        copy.start()
    return copies


def forward_lanes(points, store, twiddle_ref):
    for m, value in enumerate(butterflies(points, turn_pair(-1))):
        if m > 0:
            value = twiddle_pair(value, twiddle_ref[0, m : m + 1], twiddle_ref[1, m : m + 1], -1)
        store(m, jnp.concatenate(value, axis=1))


def first_kernel(
    in_ref, g_hbm, twiddle_hbm, out_ref, line_ref, part_ref, g_ref, twiddle_ref, sems
):
    local_harm, rows = out_ref.shape[1], out_ref.shape[2]
    lines = rows * 2 * RADIX
    copies = fetch(
        [in_ref.at[pl.ds(n * lines, lines)] for n in range(local_harm)] + [twiddle_hbm, g_hbm],
        [line_ref.at[n] for n in range(local_harm)] + [twiddle_ref, g_ref],
        sems,
    )
    copies[local_harm].wait()
    for n in range(local_harm):
        copies[n].wait()
        for start in range(0, rows, 16):
            points = [
                tuple(
                    line_ref[n, pl.ds(start * 16 + 2 * k + c, 16, stride=16), :]
                    for c in range(2)
                )
                for k in range(RADIX)
            ]

            def store(m, value):
                first = (m * local_harm + n) * rows + start
                store_parts(part_ref, slice(first, first + 16), value)

            forward_lanes(points, store, twiddle_ref)
    copies[local_harm + 1].wait()
    result = product(part_ref[...], g_ref[...])
    for m in range(RADIX):
        for n in range(local_harm):
            first = (m * local_harm + n) * rows
            out_ref[2 * m, n] = result[first : first + rows, :SUB]
            out_ref[2 * m + 1, n] = result[first : first + rows, SUB:]


IN_VMEM = pl.BlockSpec(memory_space=pltpu.VMEM)
IN_HBM = pl.BlockSpec(memory_space=pltpu.HBM)


def in_vmem(*arrays):
    return [pltpu.with_memory_space_constraint(array, pltpu.VMEM) for array in arrays]


def in_hbm(*arrays):
    return [pltpu.with_memory_space_constraint(array, pltpu.HBM) for array in arrays]


def first_transform(pressure, constants):
    local_harm, rows = pressure.shape[0], pressure.shape[1]
    lines = pressure.reshape(local_harm, rows, 2, RADIX, SUB).transpose(0, 1, 3, 2, 4)
    lines = lines.reshape(local_harm * rows * 16, SUB)
    _, _, forward, _, twiddles = constants
    return pl.pallas_call(
        first_kernel,
        in_specs=[IN_HBM] * 3,
        out_specs=IN_VMEM,
        out_shape=pltpu.VMEM((16, local_harm, rows, SUB), jnp.float32),
        scratch_shapes=[
            pltpu.VMEM((local_harm, rows * 16, SUB), jnp.float32),
            pltpu.VMEM((RADIX * local_harm * rows, 768), jnp.bfloat16),
            pltpu.VMEM(forward.shape, forward.dtype),
            pltpu.VMEM(twiddles.shape, twiddles.dtype),
            pltpu.SemaphoreType.DMA((local_harm + 2,)),
        ],
        compiler_params=pltpu.CompilerParams(vmem_limit_bytes=VMEM_LIMIT),
        cost_estimate=pl.CostEstimate(
            flops=3 * 2 * local_harm * rows * RADIX * 65536,
            bytes_accessed=2 * lines.size * 4,
            transcendentals=0,
        ),
        name="first_transform",
    )(*in_hbm(lines, forward, twiddles))


def march_kernel(by_rows, in_ref, twiddle_ref, forward_ref, inverse_ref, prop_ref, *refs):
    out_ref, line_ref, part_ref, spec_ref = refs[-4:]
    local_harm = out_ref.shape[2]

    def load(n, block):
        if by_rows:
            return [in_ref[block, n]]
        return [in_ref[tile, block, n] for tile in range(8)]

    def first_row(m, n):
        return (m * local_harm + n) * HALF

    for n in range(local_harm):
        for k in range(RADIX):
            columns = jnp.concatenate(load(n, 2 * k) + load(n, 2 * k + 1), 0)
            line_ref[n, k] = columns.T
    for n in range(local_harm):
        for start in range(0, HALF, 16):
            points = [
                tuple(
                    line_ref[n, k, HALF * c + start : HALF * c + start + 16] for c in range(2)
                )
                for k in range(RADIX)
            ]

            def store(m, value):
                first = first_row(m, n) + start
                store_parts(part_ref, slice(first, first + 16), value)

            forward_lanes(points, store, twiddle_ref)
    spec_ref[...] = product(part_ref[...], forward_ref[...])
    for m in range(RADIX):
        for n in range(local_harm):
            for start in range(0, HALF, 16):
                rows = slice(first_row(m, n) + start, first_row(m, n) + start + 16)
                tile = slice(start, start + 16)
                real, imag = spec_ref[rows, :SUB], spec_ref[rows, SUB:]
                prop_real, prop_imag = prop_ref[0, n, m, tile], prop_ref[1, n, m, tile]
                value = (
                    real * prop_real - imag * prop_imag,
                    real * prop_imag + imag * prop_real,
                )
                store_parts(part_ref, rows, jnp.concatenate(value, 1))
    spec_ref[...] = product(part_ref[...], inverse_ref[...])
    for n in range(local_harm):
        for start in range(0, HALF, 8):
            points = []
            for m in range(RADIX):
                rows = slice(first_row(m, n) + start, first_row(m, n) + start + 8)
                value = (spec_ref[rows, :SUB], spec_ref[rows, SUB:])
                if m > 0:
                    value = twiddle_pair(
                        value, twiddle_ref[0, m : m + 1], twiddle_ref[1, m : m + 1], 1
                    )
                points.append(value)
            for k, value in enumerate(butterflies(points, turn_pair(1))):
                for c in range(2):
                    line_ref[n, k, HALF * c + start : HALF * c + start + 8] = value[c]
        for k in range(RADIX):
            columns = line_ref[n, k].T
            for tile in range(16):
                out_ref[tile % 8, 2 * k + tile // 8, n] = columns[8 * tile : 8 * tile + 8]


def bring_kernel(*refs):
    count = (len(refs) - 2) // 2
    for copy in fetch(refs[:count], refs[count + 1 : -1], refs[-1]):
        copy.wait()


def bring(arrays, after):
    operands = in_hbm(*arrays) + [after]
    return pl.pallas_call(
        bring_kernel,
        in_specs=[IN_HBM] * len(arrays) + [pl.BlockSpec(memory_space=pl.ANY)],
        out_specs=[IN_VMEM] * len(arrays),
        out_shape=[pltpu.VMEM(array.shape, array.dtype) for array in arrays],
        scratch_shapes=[pltpu.SemaphoreType.DMA((len(arrays),))],
        name="bring",
    )(*operands)


def march(wavefield, prop, after, constants, by_rows):
    local_harm = wavefield.shape[1 if by_rows else 2]
    forward, inverse, _, _, twiddles = constants
    tables = [twiddles, forward, inverse]
    if by_rows:
        tables = bring(tables, prop)
    operands = in_vmem(wavefield, *tables, prop)
    in_specs = [IN_VMEM] * len(operands)
    if by_rows:
        operands += in_hbm(*after)
        in_specs += [IN_HBM] * len(after)
    scratch = [
        pltpu.VMEM((local_harm, RADIX, SUB, SUB), jnp.float32),
        pltpu.VMEM((RADIX * local_harm * HALF, 768), jnp.bfloat16),
        pltpu.VMEM((RADIX * local_harm * HALF, 2 * SUB), jnp.float32),
    ]
    return pl.pallas_call(
        functools.partial(march_kernel, by_rows),
        in_specs=in_specs,
        out_specs=IN_VMEM,
        out_shape=pltpu.VMEM((8, 16, local_harm, 8, SUB), jnp.float32),
        scratch_shapes=scratch,
        compiler_params=pltpu.CompilerParams(vmem_limit_bytes=VMEM_LIMIT),
        cost_estimate=pl.CostEstimate(
            flops=2 * 2 * local_harm * 512 * 768 * 256,
            bytes_accessed=4 * wavefield.size * 4,
            transcendentals=0,
        ),
        name="march",
    )(*operands)


class Network:
    def __init__(self, inputs):
        self.inputs = inputs
        self.terms = [()] * inputs
        self.known = {}

    def node(self, terms):
        if terms not in self.known:
            self.known[terms] = len(self.terms)
            self.terms.append(terms)
        return self.known[terms]

    def negate(self, x):
        return None if x is None else (-x[0], x[1])

    def scale(self, factor, x):
        if x is None:
            return None
        sign = x[0] if factor > 0 else -x[0]
        return (sign, self.node(((abs(factor), x[1]),)))

    def add(self, x, y):
        if x is None or y is None:
            return y if x is None else x
        if x[1] > y[1]:
            x, y = y, x
        return (x[0], self.node(((1.0, x[1]), (float(x[0] * y[0]), y[1]))))

    def subtract(self, x, y):
        return self.add(x, self.negate(y))

    def rotate(self, turns, z):
        cosine, sine = math.cos(2.0 * math.pi * turns), math.sin(2.0 * math.pi * turns)
        real, imag = z
        if turns == 0.0:
            return z
        if turns == 0.25:
            return (self.negate(imag), real)
        if turns == 0.125:
            return (
                self.scale(cosine, self.subtract(real, imag)),
                self.scale(cosine, self.add(imag, real)),
            )
        return (
            self.subtract(self.scale(cosine, real), self.scale(sine, imag)),
            self.add(self.scale(cosine, imag), self.scale(sine, real)),
        )

    def five_points(self, x):
        def both(operation, a, b):
            return (operation(a[0], b[0]), operation(a[1], b[1]))

        def times(factor, a):
            return (self.scale(factor, a[0]), self.scale(factor, a[1]))

        def turned(a):
            return (self.negate(a[1]), a[0])

        plus, minus = self.add, self.subtract
        sum_1, sum_2 = both(plus, x[1], x[4]), both(plus, x[2], x[3])
        diff_1, diff_2 = both(minus, x[1], x[4]), both(minus, x[2], x[3])
        total, gap = both(plus, sum_1, sum_2), both(minus, sum_1, sum_2)
        base, step = both(plus, x[0], times(-0.25, total)), times(math.sqrt(5.0) / 4.0, gap)
        even_1, even_2 = both(plus, base, step), both(minus, base, step)
        sine_1, sine_2 = math.sin(0.4 * math.pi), math.sin(0.8 * math.pi)
        odd_1 = turned(both(plus, times(sine_1, diff_1), times(sine_2, diff_2)))
        odd_2 = turned(both(minus, times(sine_2, diff_1), times(sine_1, diff_2)))
        return [
            both(plus, x[0], total),
            both(plus, even_1, odd_1),
            both(plus, even_2, odd_2),
            both(minus, even_2, odd_2),
            both(minus, even_1, odd_1),
        ]

    def real_points(self, u, length):
        if length == 1:
            return [u[0][0]]
        half = length // 2
        out = [None] * length
        for odd in range(2):
            folded = {}
            for k, z in u.items():
                z = self.rotate(k * odd / length, z)
                k %= half
                if 2 * k > half:
                    k, z = half - k, (z[0], self.negate(z[1]))
                old = folded.get(k, (None, None))
                folded[k] = (self.add(old[0], z[0]), self.add(old[1], z[1]))
            for k in folded:
                if k == 0 or 2 * k == half:
                    folded[k] = (folded[k][0], None)
            out[odd::2] = self.real_points(folded, half)
        return out


def sample_network():
    assert 3 * H < 80
    network = Network(2 * H)
    grid = [[(None, None)] * 5 for _ in range(9)]
    for n in range(1, H + 1):
        real, imag = (1, 2 * n - 2), (1, 2 * n - 1)
        k, place = n % 16, n % 5
        if k > 8:
            k, place, imag = 16 - k, -n % 5, network.negate(imag)
        grid[k][place] = (real, imag)
    columns = [network.five_points(row) for row in grid]
    groups = []
    for instant in range(5):
        start = len(network.terms)
        u = {k: columns[k][instant] for k in range(9)}
        u[0], u[8] = (u[0][0], None), (u[8][0], None)
        groups.append((start, network.real_points(u, 16)))
    return network, groups


def signed_sum(old, sign, value):
    if old is None:
        return (sign, value)
    if old[0] == sign:
        return (sign, old[1] + value)
    return (1, old[1] - value) if old[0] > 0 else (1, value - old[1])


def couple_pixels(load, gain, store):
    network, groups = sample_network()
    values = {}

    def value(node):
        if node not in values:
            if node < network.inputs:
                values[node] = load(node)
            else:
                terms = network.terms[node]
                first = value(terms[0][1])
                if len(terms) == 1:
                    values[node] = terms[0][0] * first
                else:
                    second = value(terms[1][1])
                    values[node] = first + second if terms[1][0] > 0 else first - second
        return values[node]

    sums = [None] * len(network.terms)
    end = len(network.terms)
    for start, outputs in reversed([(network.inputs, [])] + groups):
        for sign, node in outputs:
            sample = value(node)
            sums[node] = signed_sum(sums[node], sign, sample * sample)
        for node in range(end - 1, start - 1, -1):
            if sums[node] is None:
                continue
            sign, total = sums[node]
            for factor, source in network.terms[node]:
                if abs(factor) == 1.0:
                    part = (sign if factor > 0 else -sign, total)
                else:
                    part = (sign, factor * total)
                sums[source] = signed_sum(sums[source], *part)
        end = start
    for n in range(1, H + 1):
        weight = (n * 4.0 / 80.0) * gain
        (sign_real, real), (sign_imag, imag) = sums[2 * n - 2], sums[2 * n - 1]
        old_real, old_imag = load(2 * n - 2), load(2 * n - 1)
        turn_real, turn_imag = weight * imag, weight * real
        store(
            n,
            old_real - turn_real if sign_imag > 0 else old_real + turn_real,
            old_imag + turn_imag if sign_real > 0 else old_imag - turn_imag,
        )


def pixel_kernel(
    last,
    in_ref,
    inverse_ref,
    twiddle_ref,
    screen_ref,
    gain_ref,
    forward_ref,
    out_ref,
    part_ref,
    line_ref,
    field_ref,
):
    local_harm = H // 8
    height = 8 * H

    def tile_of(n, r):
        return in_ref[n // local_harm, r, n % local_harm]

    for n in range(0, H, 2):
        for m in range(RADIX):
            value = jnp.concatenate(
                [
                    jnp.concatenate([tile_of(n + i, 2 * m), tile_of(n + i, 2 * m + 1)], 1)
                    for i in range(2)
                ],
                0,
            )
            first = height * m + 8 * n
            store_parts(part_ref, slice(first, first + 16), value)
    line_ref[...] = product(part_ref[...], inverse_ref[...])

    for n in range(H):
        points = []
        for m in range(RADIX):
            rows = slice(height * m + 8 * n, height * m + 8 * n + 8)
            value = (line_ref[rows, :SUB], line_ref[rows, SUB:])
            if m > 0:
                value = twiddle_pair(value, twiddle_ref[0, m : m + 1], twiddle_ref[1, m : m + 1], 1)
            points.append(value)
        for k, (real, imag) in enumerate(butterflies(points, turn_pair(1))):
            lanes = slice(SUB * k, SUB * k + SUB)
            factor_real, factor_imag = screen_ref[0, n, :, lanes], screen_ref[1, n, :, lanes]
            field_ref[k, 2 * n] = real * factor_real - imag * factor_imag
            field_ref[k, 2 * n + 1] = real * factor_imag + imag * factor_real

    def one_block(k, carry):
        def load(index):
            return field_ref[k, index]

        def store(n, real, imag):
            if last:
                start = 128 * (n - 1) + 2 * k
                out_ref[pl.ds(start, 8, stride=16), :] = real
                out_ref[pl.ds(start + 1, 8, stride=16), :] = imag
            else:
                rows = pl.ds(pl.multiple_of(height * k + 8 * n - 8, 8), 8)
                line_ref[rows, :SUB] = real
                line_ref[rows, SUB:] = imag

        couple_pixels(load, gain_ref[k], store)
        return carry

    lax.fori_loop(0, RADIX, one_block, 0)
    if last:
        return

    for n in range(0, H, 2):

        def rows(block, n=n):
            return slice(height * block + 8 * n, height * block + 8 * n + 16)

        points = [(line_ref[rows(k), :SUB], line_ref[rows(k), SUB:]) for k in range(RADIX)]
        forward_lanes(
            points, lambda m, value: store_parts(part_ref, rows(m), value), twiddle_ref
        )
    result = product(part_ref[...], forward_ref[...])
    for m in range(RADIX):
        for n in range(H):
            first = height * m + 8 * n
            for half in range(2):
                out_ref[n // local_harm, 2 * m + half, n % local_harm] = result[
                    first : first + 8, SUB * half : SUB * half + SUB
                ]


def pixels(wavefield, screen, gain, constants, last):
    _, _, forward, inverse, twiddles = constants
    tables = [inverse, twiddles, screen, gain, forward]
    operands = in_vmem(wavefield, *tables)
    out_shape = (H * 8 * 16, SUB) if last else wavefield.shape
    return pl.pallas_call(
        functools.partial(pixel_kernel, last),
        in_specs=[IN_VMEM] * len(operands),
        out_specs=IN_VMEM,
        out_shape=pltpu.VMEM(out_shape, jnp.float32),
        scratch_shapes=[
            pltpu.VMEM((RADIX * 8 * H, 768), jnp.bfloat16),
            pltpu.VMEM((RADIX * 8 * H, 2 * SUB), jnp.float32),
            pltpu.VMEM((RADIX, 2 * H, 8, SUB), jnp.float32),
        ],
        compiler_params=pltpu.CompilerParams(vmem_limit_bytes=VMEM_LIMIT),
        cost_estimate=pl.CostEstimate(
            flops=2 * 3 * 2 * 8 * H * RADIX * 65536,
            bytes_accessed=4 * wavefield.size * 4,
            transcendentals=0,
        ),
        name="pixels_last" if last else "pixels",
    )(*operands)


def order_kernel(in_ref, out_ref, sems):
    groups, local_harm = in_ref.shape[:2]
    pairs = [(h, n) for h in range(groups) for n in range(local_harm)]
    copies = fetch(
        [in_ref.at[h, n] for h, n in pairs], [out_ref.at[n, h] for h, n in pairs], sems
    )
    for copy in copies:
        copy.wait()


def order_rows(blocks):
    groups, local_harm = blocks.shape[:2]
    return pl.pallas_call(
        order_kernel,
        in_specs=[IN_VMEM],
        out_specs=IN_HBM,
        out_shape=jax.ShapeDtypeStruct((local_harm, groups) + blocks.shape[2:], blocks.dtype),
        scratch_shapes=[pltpu.SemaphoreType.DMA((groups * local_harm,))],
        name="order_rows",
    )(*in_vmem(blocks))


def squared_freq_at(indices, length):
    centred = jnp.where(indices < length // 2, indices, indices - length).astype(jnp.float32)
    scaled = centred * (2.0 * math.pi / length)
    return scaled * scaled


def propagator(wave_number, down_square, across_square, march_step):
    axial_square = wave_number * wave_number - down_square - across_square
    axial_root = jnp.sqrt(jnp.abs(axial_square))
    phase_turn = march_step * axial_root
    propagating = axial_square >= 0.0
    prop_real = jnp.where(propagating, jnp.cos(phase_turn), jnp.exp(-phase_turn))
    prop_imag = jnp.where(propagating, jnp.sin(phase_turn), 0.0)
    return (prop_real, prop_imag)


def propagator_tables(local_harm):
    orders = (
        lax.axis_index("harm") * local_harm + jnp.arange(local_harm, dtype=jnp.int32) + 1
    ).astype(jnp.float32)
    place = lax.axis_index("rows")
    down = RADIX * jnp.arange(SUB, dtype=jnp.int32)[None, :] + jnp.arange(
        RADIX, dtype=jnp.int32
    )[:, None]
    across = (
        RADIX * (lax.rem(place, 2) * HALF + jnp.arange(HALF, dtype=jnp.int32)) + place // 2
    )
    real, imag = propagator(
        (3.0 / H * orders)[:, None, None, None],
        squared_freq_at(down, N)[None, :, None, :],
        squared_freq_at(across, N)[None, None, :, None],
        float(DZ),
    )
    return jnp.stack([real, imag]) * (1.0 / (N * N))


def screen_tables(contrast, absorption):
    orders = jnp.arange(1, H + 1, dtype=jnp.int32).astype(jnp.float32)[:, None, None]
    damping = jnp.exp(-absorption[None] * jnp.power(orders, 1.1) * float(DZ))
    angle = 3.0 / H * orders * float(DZ) * contrast[None]
    return jnp.stack([damping * jnp.cos(angle), damping * jnp.sin(angle)])


def make_constants():
    return tuple(jnp.asarray(table) for table in lane_matrices() + (lane_twiddles(),))


def shards(pressure, contrast, absorption, nonlinearity):
    local_harm = pressure.shape[0]
    constants = make_constants()
    axes = ("harm", "rows")
    pixel_rows = 8
    row_start = lax.axis_index("harm") * pixel_rows

    def own_rows(values):
        return lax.dynamic_slice_in_dim(values, row_start, pixel_rows, 0)

    gain = own_rows(nonlinearity) * (1.0 / (H * math.sqrt(H)))
    gain = gain.reshape(pixel_rows, RADIX, SUB).transpose(1, 0, 2)
    prop = propagator_tables(local_harm)
    screen = screen_tables(own_rows(contrast), own_rows(absorption))

    lines = first_transform(pressure, constants)
    lines = lax.all_to_all(lines, "rows", 0, 0, tiled=True)
    for plane_index in range(PLANES):
        marched = march(lines, prop, (screen, gain), constants, plane_index == 0)
        shape = marched.shape
        marched = lax.all_to_all(marched.reshape((128,) + shape[2:]), axes, 0, 0, tiled=True)
        last = plane_index == PLANES - 1
        lines = pixels(marched.reshape(shape), screen, gain, constants, last)
        if not last:
            lines = lax.all_to_all(lines.reshape((128,) + shape[2:]), axes, 0, 0, tiled=True)
            lines = lines.reshape(shape)
    out = lines.reshape(8, local_harm, pixel_rows * 16, SUB)
    out = lax.all_to_all(out, "harm", 0, 0, tiled=True)
    out = order_rows(out).reshape(local_harm, 8 * pixel_rows, RADIX, 2, SUB)
    return out.transpose(0, 1, 3, 2, 4).reshape(local_harm, 8 * pixel_rows, 2, N)


def solution(mesh):
    in_specs = (P("harm", "rows", None, None), P("rows", None), P("rows", None), P("rows", None))
    out_specs = P("harm", "rows", None, None)
    return jax.shard_map(shards, mesh=mesh, in_specs=in_specs, out_specs=out_specs, check_vma=False)
```

```python
import functools
import math

import jax
import jax.numpy as jnp
import ml_dtypes
import numpy as np
from jax import lax
from jax.experimental import pallas as pl
from jax.experimental.pallas import tpu as pltpu
from jax.sharding import PartitionSpec as P

H = 24
N = 1024
PLANES = 2
DZ = 128
RADIX = 8
SUB = N // RADIX
HALF = SUB // 2
ROOT_HALF = math.sqrt(0.5)
VMEM_LIMIT = 20 * 1024 * 1024


def split_constant(table):
    high = table.astype(np.float32).astype(ml_dtypes.bfloat16)
    low = (table - high.astype(np.float64)).astype(np.float32).astype(ml_dtypes.bfloat16)
    return high, low


def stack_constant(table):
    high, low = split_constant(table)
    return np.concatenate([high, high, low], 0)


def sub_angles():
    index = np.arange(SUB)
    return 2.0 * np.pi / SUB * ((index[:, None] * index[None, :]) % SUB)


def lane_matrices():
    cosine, sine = np.cos(sub_angles()), np.sin(sub_angles())
    forward = np.block([[cosine, -sine], [sine, cosine]])
    inverse = np.block([[cosine, sine], [-sine, cosine]])
    order = np.arange(2 * SUB).reshape(2, 2, HALF).transpose(1, 0, 2).reshape(-1)
    tables = (forward, inverse, forward[:, order], inverse[order])
    return tuple(stack_constant(table) for table in tables)


def lane_twiddles():
    angle = 2.0 * np.pi / N * (np.arange(RADIX)[:, None] * np.arange(SUB)[None, :])
    return np.stack([np.cos(angle), np.sin(angle)]).astype(np.float32)


def split_value(value):
    high = value.astype(jnp.bfloat16)
    low = (value - high.astype(jnp.float32)).astype(jnp.bfloat16)
    return high, low


def add(left, right):
    return tuple(a + b for a, b in zip(left, right))


def subtract(left, right):
    return tuple(a - b for a, b in zip(left, right))


def scale(value, factor):
    return tuple(a * factor for a in value)


def turn_pair(direction):
    def turn(value):
        real, imag = value
        return (imag, -real) if direction < 0 else (-imag, real)

    return turn


def butterflies(points, turn):
    even = [add(points[k], points[k + 4]) for k in range(4)]
    odd = [subtract(points[k], points[k + 4]) for k in range(4)]
    turned = turn(odd[1])
    first = scale(add(odd[1], turned), ROOT_HALF)
    second = turn(odd[2])
    turned = turn(odd[3])
    third = scale(subtract(turned, odd[3]), ROOT_HALF)
    out = [None] * RADIX
    for offset, (a, b, c, d) in ((0, even), (1, (odd[0], first, second, third))):
        sum_ac, diff_ac = add(a, c), subtract(a, c)
        sum_bd, diff_bd = add(b, d), turn(subtract(b, d))
        out[offset] = add(sum_ac, sum_bd)
        out[offset + 4] = subtract(sum_ac, sum_bd)
        out[offset + 2] = add(diff_ac, diff_bd)
        out[offset + 6] = subtract(diff_ac, diff_bd)
    return out


def product(left, right):
    return jnp.dot(left, right, preferred_element_type=jnp.float32)


def store_parts(part_ref, rows, value):
    high, low = split_value(value)
    part_ref[rows, :256] = high
    part_ref[rows, 256:512] = low
    part_ref[rows, 512:] = high


def twiddle_pair(value, cosine, sine, direction):
    real, imag = value
    if direction < 0:
        return real * cosine + imag * sine, imag * cosine - real * sine
    return real * cosine - imag * sine, imag * cosine + real * sine


def fetch(sources, targets, sems):
    copies = [
        pltpu.make_async_copy(source, target, sems.at[index])
        for index, (source, target) in enumerate(zip(sources, targets))
    ]
    for copy in copies:
        copy.start()
    return copies


def forward_lanes(points, store, twiddle_ref):
    for m, value in enumerate(butterflies(points, turn_pair(-1))):
        if m > 0:
            value = twiddle_pair(value, twiddle_ref[0, m : m + 1], twiddle_ref[1, m : m + 1], -1)
        store(m, jnp.concatenate(value, axis=1))


def first_kernel(
    in_ref,
    g_hbm,
    twiddle_hbm,
    out_hbm,
    line_ref,
    part_ref,
    result_ref,
    g_ref,
    twiddle_ref,
    sems,
    out_sems,
):
    local_harm, rows = line_ref.shape[0], result_ref.shape[2]
    lines = rows * 2 * RADIX
    copies = fetch(
        [in_ref.at[pl.ds(n * lines, lines)] for n in range(local_harm)] + [twiddle_hbm, g_hbm],
        [line_ref.at[n] for n in range(local_harm)] + [twiddle_ref, g_ref],
        sems,
    )
    copies[local_harm].wait()
    out_copies = []
    for n in range(local_harm):
        copies[n].wait()
        for start in range(0, rows, 16):
            points = [
                tuple(
                    line_ref[n, pl.ds(start * 16 + 2 * k + c, 16, stride=16), :]
                    for c in range(2)
                )
                for k in range(RADIX)
            ]

            def store(m, value):
                first = m * rows + start
                store_parts(part_ref.at[n], slice(first, first + 16), value)

            forward_lanes(points, store, twiddle_ref)
        if n == 0:
            copies[local_harm + 1].wait()
        result = product(part_ref[n], g_ref[...])
        for m in range(RADIX):
            for half in range(2):
                result_ref[n, 2 * m + half] = result[
                    rows * m : rows * m + rows, SUB * half : SUB * half + SUB
                ]
        copy = pltpu.make_async_copy(result_ref.at[n], out_hbm.at[:, n], out_sems.at[n])
        copy.start()
        out_copies.append(copy)
    for copy in out_copies:
        copy.wait()


IN_VMEM = pl.BlockSpec(memory_space=pltpu.VMEM)
IN_HBM = pl.BlockSpec(memory_space=pltpu.HBM)


def in_vmem(*arrays):
    return [pltpu.with_memory_space_constraint(array, pltpu.VMEM) for array in arrays]


def in_hbm(*arrays):
    return [pltpu.with_memory_space_constraint(array, pltpu.HBM) for array in arrays]


def first_transform(pressure, constants):
    local_harm, rows = pressure.shape[0], pressure.shape[1]
    lines = pressure.reshape(local_harm, rows, 2, RADIX, SUB).transpose(0, 1, 3, 2, 4)
    lines = lines.reshape(local_harm * rows * 16, SUB)
    _, _, forward, _, twiddles = constants
    return pl.pallas_call(
        first_kernel,
        in_specs=[IN_HBM] * 3,
        out_specs=IN_HBM,
        out_shape=jax.ShapeDtypeStruct((16, local_harm, rows, SUB), jnp.float32),
        scratch_shapes=[
            pltpu.VMEM((local_harm, rows * 16, SUB), jnp.float32),
            pltpu.VMEM((local_harm, RADIX * rows, 768), jnp.bfloat16),
            pltpu.VMEM((local_harm, 16, rows, SUB), jnp.float32),
            pltpu.VMEM(forward.shape, forward.dtype),
            pltpu.VMEM(twiddles.shape, twiddles.dtype),
            pltpu.SemaphoreType.DMA((local_harm + 2,)),
            pltpu.SemaphoreType.DMA((local_harm,)),
        ],
        compiler_params=pltpu.CompilerParams(vmem_limit_bytes=VMEM_LIMIT),
        cost_estimate=pl.CostEstimate(
            flops=3 * 2 * local_harm * rows * RADIX * 65536,
            bytes_accessed=2 * lines.size * 4,
            transcendentals=0,
        ),
        name="first_transform",
    )(*in_hbm(lines, forward, twiddles))


def march_kernel(by_rows, in_ref, twiddle_ref, forward_ref, inverse_ref, prop_ref, *refs):
    out_ref, line_ref, part_ref, spec_ref, back_ref = refs[-5:]
    local_harm = out_ref.shape[2]

    def load(n, block):
        if by_rows:
            return [in_ref[block, n]]
        return [in_ref[tile, block, n] for tile in range(8)]

    part = HALF // 2
    middle = RADIX * local_harm * part
    halves = [slice(half * middle, (half + 1) * middle) for half in range(2)]

    def rows_of(m, n, start, count):
        half, start = divmod(start, part)
        first = half * middle + (m * local_harm + n) * part + start
        return slice(first, first + count)

    def starts(half, count):
        return range(half * part, (half + 1) * part, count)

    def spread(half):
        for n in range(local_harm):
            for start in starts(half, 16):
                points = [
                    tuple(
                        line_ref[n, k, HALF * c + start : HALF * c + start + 16]
                        for c in range(2)
                    )
                    for k in range(RADIX)
                ]
                forward_lanes(
                    points,
                    lambda m, value: store_parts(part_ref, rows_of(m, n, start, 16), value),
                    twiddle_ref,
                )

    def propagate(half):
        for m in range(RADIX):
            for n in range(local_harm):
                for start in starts(half, 16):
                    rows = rows_of(m, n, start, 16)
                    tile = slice(start, start + 16)
                    real, imag = spec_ref[rows, :SUB], spec_ref[rows, SUB:]
                    prop_real, prop_imag = prop_ref[0, n, m, tile], prop_ref[1, n, m, tile]
                    value = (
                        real * prop_real - imag * prop_imag,
                        real * prop_imag + imag * prop_real,
                    )
                    store_parts(part_ref, rows, jnp.concatenate(value, 1))

    def gather(half, n):
        for start in starts(half, 8):
            points = []
            for m in range(RADIX):
                rows = rows_of(m, n, start, 8)
                value = (back_ref[rows, :SUB], back_ref[rows, SUB:])
                if m > 0:
                    value = twiddle_pair(
                        value, twiddle_ref[0, m : m + 1], twiddle_ref[1, m : m + 1], 1
                    )
                points.append(value)
            for k, value in enumerate(butterflies(points, turn_pair(1))):
                for c in range(2):
                    line_ref[n, k, HALF * c + start : HALF * c + start + 8] = value[c]

    for n in range(local_harm):
        for k in range(RADIX):
            columns = jnp.concatenate(load(n, 2 * k) + load(n, 2 * k + 1), 0)
            line_ref[n, k] = columns.T
    first, second = halves
    spread(0)
    spec_ref[first] = product(part_ref[first], forward_ref[...])
    spread(1)
    spec_ref[second] = product(part_ref[second], forward_ref[...])
    propagate(0)
    back_ref[first] = product(part_ref[first], inverse_ref[...])
    propagate(1)
    back_ref[second] = product(part_ref[second], inverse_ref[...])
    for n in range(local_harm):
        gather(0, n)
    for n in range(local_harm):
        gather(1, n)
        for k in range(RADIX):
            columns = line_ref[n, k].T
            for tile in range(16):
                out_ref[tile % 8, 2 * k + tile // 8, n] = columns[8 * tile : 8 * tile + 8]


def bring_kernel(*refs):
    count = 3
    for copy in fetch(refs[:count], refs[-count - 1 : -1], refs[-1]):
        copy.wait()


def bring(arrays, after):
    operands = in_hbm(*arrays) + list(after)
    return pl.pallas_call(
        bring_kernel,
        in_specs=[IN_HBM] * len(arrays) + [pl.BlockSpec(memory_space=pl.ANY)] * len(after),
        out_specs=[IN_VMEM] * len(arrays),
        out_shape=[pltpu.VMEM(array.shape, array.dtype) for array in arrays],
        scratch_shapes=[pltpu.SemaphoreType.DMA((len(arrays),))],
        name="bring",
    )(*operands)


def march(wavefield, prop, after, constants, by_rows):
    local_harm = wavefield.shape[1 if by_rows else 2]
    forward, inverse, _, _, twiddles = constants
    tables = [twiddles, forward, inverse]
    if by_rows:
        tables = bring(tables, after[:1])
    operands = in_vmem(wavefield, *tables, prop)
    in_specs = [IN_VMEM] * len(operands)
    if by_rows:
        operands += in_hbm(*after)
        in_specs += [IN_HBM] * len(after)
    scratch = [
        pltpu.VMEM((local_harm, RADIX, SUB, SUB), jnp.float32),
        pltpu.VMEM((RADIX * local_harm * HALF, 768), jnp.bfloat16),
        pltpu.VMEM((RADIX * local_harm * HALF, 2 * SUB), jnp.float32),
        pltpu.VMEM((RADIX * local_harm * HALF, 2 * SUB), jnp.float32),
    ]
    return pl.pallas_call(
        functools.partial(march_kernel, by_rows),
        in_specs=in_specs,
        out_specs=IN_VMEM,
        out_shape=pltpu.VMEM((8, 16, local_harm, 8, SUB), jnp.float32),
        scratch_shapes=scratch,
        compiler_params=pltpu.CompilerParams(vmem_limit_bytes=VMEM_LIMIT),
        cost_estimate=pl.CostEstimate(
            flops=2 * 2 * local_harm * 512 * 768 * 256,
            bytes_accessed=4 * wavefield.size * 4,
            transcendentals=0,
        ),
        name="march",
    )(*operands)


class Network:
    def __init__(self, inputs):
        self.inputs = inputs
        self.terms = [()] * inputs
        self.known = {}

    def node(self, terms):
        if terms not in self.known:
            self.known[terms] = len(self.terms)
            self.terms.append(terms)
        return self.known[terms]

    def negate(self, x):
        return None if x is None else (-x[0], x[1])

    def scale(self, factor, x):
        if x is None:
            return None
        sign = x[0] if factor > 0 else -x[0]
        return (sign, self.node(((abs(factor), x[1]),)))

    def add(self, x, y):
        if x is None or y is None:
            return y if x is None else x
        if x[1] > y[1]:
            x, y = y, x
        return (x[0], self.node(((1.0, x[1]), (float(x[0] * y[0]), y[1]))))

    def subtract(self, x, y):
        return self.add(x, self.negate(y))

    def rotate(self, turns, z):
        cosine, sine = math.cos(2.0 * math.pi * turns), math.sin(2.0 * math.pi * turns)
        real, imag = z
        if turns == 0.0:
            return z
        if turns == 0.25:
            return (self.negate(imag), real)
        if turns == 0.125:
            return (
                self.scale(cosine, self.subtract(real, imag)),
                self.scale(cosine, self.add(imag, real)),
            )
        return (
            self.subtract(self.scale(cosine, real), self.scale(sine, imag)),
            self.add(self.scale(cosine, imag), self.scale(sine, real)),
        )

    def five_points(self, x):
        def both(operation, a, b):
            return (operation(a[0], b[0]), operation(a[1], b[1]))

        def times(factor, a):
            return (self.scale(factor, a[0]), self.scale(factor, a[1]))

        def turned(a):
            return (self.negate(a[1]), a[0])

        plus, minus = self.add, self.subtract
        sum_1, sum_2 = both(plus, x[1], x[4]), both(plus, x[2], x[3])
        diff_1, diff_2 = both(minus, x[1], x[4]), both(minus, x[2], x[3])
        total, gap = both(plus, sum_1, sum_2), both(minus, sum_1, sum_2)
        base, step = both(plus, x[0], times(-0.25, total)), times(math.sqrt(5.0) / 4.0, gap)
        even_1, even_2 = both(plus, base, step), both(minus, base, step)
        sine_1, sine_2 = math.sin(0.4 * math.pi), math.sin(0.8 * math.pi)
        odd_1 = turned(both(plus, times(sine_1, diff_1), times(sine_2, diff_2)))
        odd_2 = turned(both(minus, times(sine_2, diff_1), times(sine_1, diff_2)))
        return [
            both(plus, x[0], total),
            both(plus, even_1, odd_1),
            both(plus, even_2, odd_2),
            both(minus, even_2, odd_2),
            both(minus, even_1, odd_1),
        ]

    def real_points(self, u, length):
        if length == 1:
            return [u[0][0]]
        half = length // 2
        out = [None] * length
        for odd in range(2):
            folded = {}
            for k, z in u.items():
                z = self.rotate(k * odd / length, z)
                k %= half
                if 2 * k > half:
                    k, z = half - k, (z[0], self.negate(z[1]))
                old = folded.get(k, (None, None))
                folded[k] = (self.add(old[0], z[0]), self.add(old[1], z[1]))
            for k in folded:
                if k == 0 or 2 * k == half:
                    folded[k] = (folded[k][0], None)
            out[odd::2] = self.real_points(folded, half)
        return out


def sample_network():
    assert 3 * H < 80
    network = Network(2 * H)
    grid = [[(None, None)] * 5 for _ in range(9)]
    for n in range(1, H + 1):
        real, imag = (1, 2 * n - 2), (1, 2 * n - 1)
        k, place = n % 16, n % 5
        if k > 8:
            k, place, imag = 16 - k, -n % 5, network.negate(imag)
        grid[k][place] = (real, imag)
    columns = [network.five_points(row) for row in grid]
    groups = []
    for instant in range(5):
        start = len(network.terms)
        u = {k: columns[k][instant] for k in range(9)}
        u[0], u[8] = (u[0][0], None), (u[8][0], None)
        groups.append((start, network.real_points(u, 16)))
    return network, groups


def signed_sum(old, sign, value):
    if old is None:
        return (sign, value)
    if old[0] == sign:
        return (sign, old[1] + value)
    return (1, old[1] - value) if old[0] > 0 else (1, value - old[1])


def couple_pixels(load, gain, store):
    network, groups = sample_network()
    values = {}

    def value(node):
        if node not in values:
            if node < network.inputs:
                values[node] = load(node)
            else:
                terms = network.terms[node]
                first = value(terms[0][1])
                if len(terms) == 1:
                    values[node] = terms[0][0] * first
                else:
                    second = value(terms[1][1])
                    values[node] = first + second if terms[1][0] > 0 else first - second
        return values[node]

    sums = [None] * len(network.terms)
    end = len(network.terms)
    for start, outputs in reversed([(network.inputs, [])] + groups):
        for sign, node in outputs:
            sample = value(node)
            sums[node] = signed_sum(sums[node], sign, sample * sample)
        for node in range(end - 1, start - 1, -1):
            if sums[node] is None:
                continue
            sign, total = sums[node]
            for factor, source in network.terms[node]:
                if abs(factor) == 1.0:
                    part = (sign if factor > 0 else -sign, total)
                else:
                    part = (sign, factor * total)
                sums[source] = signed_sum(sums[source], *part)
        end = start
    for n in range(1, H + 1):
        weight = (n * 4.0 / 80.0) * gain
        (sign_real, real), (sign_imag, imag) = sums[2 * n - 2], sums[2 * n - 1]
        old_real, old_imag = load(2 * n - 2), load(2 * n - 1)
        turn_real, turn_imag = weight * imag, weight * real
        store(
            n,
            old_real - turn_real if sign_imag > 0 else old_real + turn_real,
            old_imag + turn_imag if sign_real > 0 else old_imag - turn_imag,
        )


def pixel_kernel(
    last,
    in_ref,
    inverse_ref,
    twiddle_ref,
    screen_ref,
    gain_ref,
    forward_ref,
    out_ref,
    part_ref,
    line_ref,
    field_ref,
):
    local_harm = H // 8
    part = H // 2
    height = 8 * part
    middle = RADIX * height
    halves = [slice(half * middle, (half + 1) * middle) for half in range(2)]

    def orders(half, step):
        return range(half * part, (half + 1) * part, step)

    def rows_of(block, n, count):
        half, n = divmod(n, part)
        first = half * middle + height * block + 8 * n
        return slice(first, first + count)

    def tile_of(n, r):
        return in_ref[n // local_harm, r, n % local_harm]

    def split_half(half):
        for n in orders(half, 2):
            for m in range(RADIX):
                value = jnp.concatenate(
                    [
                        jnp.concatenate([tile_of(n + i, 2 * m), tile_of(n + i, 2 * m + 1)], 1)
                        for i in range(2)
                    ],
                    0,
                )
                store_parts(part_ref, rows_of(m, n, 16), value)

    def screen_half(half):
        for n in orders(half, 1):
            points = []
            for m in range(RADIX):
                rows = rows_of(m, n, 8)
                value = (line_ref[rows, :SUB], line_ref[rows, SUB:])
                if m > 0:
                    value = twiddle_pair(
                        value, twiddle_ref[0, m : m + 1], twiddle_ref[1, m : m + 1], 1
                    )
                points.append(value)
            for k, (real, imag) in enumerate(butterflies(points, turn_pair(1))):
                lanes = slice(SUB * k, SUB * k + SUB)
                factor_real, factor_imag = screen_ref[0, n, :, lanes], screen_ref[1, n, :, lanes]
                field_ref[k, 2 * n] = real * factor_real - imag * factor_imag
                field_ref[k, 2 * n + 1] = real * factor_imag + imag * factor_real

    first, second = halves
    split_half(0)
    line_ref[first] = product(part_ref[first], inverse_ref[...])
    split_half(1)
    line_ref[second] = product(part_ref[second], inverse_ref[...])
    screen_half(0)
    screen_half(1)

    def one_block(k, carry):
        def load(index):
            return field_ref[k, index]

        def store(n, real, imag):
            if last:
                start = 128 * (n - 1) + 2 * k
                out_ref[pl.ds(start, 8, stride=16), :] = real
                out_ref[pl.ds(start + 1, 8, stride=16), :] = imag
            else:
                field_ref[k, 2 * n - 2] = real
                field_ref[k, 2 * n - 1] = imag

        couple_pixels(load, gain_ref[k], store)
        return carry

    lax.fori_loop(0, RADIX, one_block, 0)
    if last:
        return

    def spread_half(half):
        for n in orders(half, 2):
            points = [
                tuple(
                    jnp.concatenate([field_ref[k, 2 * n + c], field_ref[k, 2 * n + 2 + c]], 0)
                    for c in range(2)
                )
                for k in range(RADIX)
            ]
            forward_lanes(
                points,
                lambda m, value: store_parts(part_ref, rows_of(m, n, 16), value),
                twiddle_ref,
            )

    def store_half(half):
        result = product(part_ref[halves[half]], forward_ref[...])
        for m in range(RADIX):
            for n in orders(half, 1):
                row = height * m + 8 * (n - half * part)
                for side in range(2):
                    out_ref[n // local_harm, 2 * m + side, n % local_harm] = result[
                        row : row + 8, SUB * side : SUB * side + SUB
                    ]

    spread_half(0)
    store_half(0)
    spread_half(1)
    store_half(1)


def pixels(wavefield, screen, gain, constants, last):
    _, _, forward, inverse, twiddles = constants
    tables = [inverse, twiddles, screen, gain, forward]
    operands = in_vmem(wavefield, *tables)
    out_shape = (H * 8 * 16, SUB) if last else wavefield.shape
    return pl.pallas_call(
        functools.partial(pixel_kernel, last),
        in_specs=[IN_VMEM] * len(operands),
        out_specs=IN_VMEM,
        out_shape=pltpu.VMEM(out_shape, jnp.float32),
        scratch_shapes=[
            pltpu.VMEM((RADIX * 8 * H, 768), jnp.bfloat16),
            pltpu.VMEM((RADIX * 8 * H, 2 * SUB), jnp.float32),
            pltpu.VMEM((RADIX, 2 * H, 8, SUB), jnp.float32),
        ],
        compiler_params=pltpu.CompilerParams(vmem_limit_bytes=VMEM_LIMIT),
        cost_estimate=pl.CostEstimate(
            flops=2 * 3 * 2 * 8 * H * RADIX * 65536,
            bytes_accessed=4 * wavefield.size * 4,
            transcendentals=0,
        ),
        name="pixels_last" if last else "pixels",
    )(*operands)


def order_kernel(in_ref, out_ref, sems):
    orders = range(in_ref.shape[1])
    copies = fetch([in_ref.at[:, n] for n in orders], [out_ref.at[n] for n in orders], sems)
    for copy in copies:
        copy.wait()


def order_rows(blocks):
    groups, local_harm = blocks.shape[:2]
    return pl.pallas_call(
        order_kernel,
        in_specs=[IN_VMEM],
        out_specs=IN_HBM,
        out_shape=jax.ShapeDtypeStruct((local_harm, groups) + blocks.shape[2:], blocks.dtype),
        scratch_shapes=[pltpu.SemaphoreType.DMA((local_harm,))],
        name="order_rows",
    )(*in_vmem(blocks))


def squared_freq_at(indices, length):
    centred = jnp.where(indices < length // 2, indices, indices - length).astype(jnp.float32)
    scaled = centred * (2.0 * math.pi / length)
    return scaled * scaled


def propagator(wave_number, down_square, across_square, march_step):
    axial_square = wave_number * wave_number - down_square - across_square
    axial_root = jnp.sqrt(jnp.abs(axial_square))
    phase_turn = march_step * axial_root
    propagating = axial_square >= 0.0
    prop_real = jnp.where(propagating, jnp.cos(phase_turn), jnp.exp(-phase_turn))
    prop_imag = jnp.where(propagating, jnp.sin(phase_turn), 0.0)
    return (prop_real, prop_imag)


def propagator_tables(local_harm):
    orders = (
        lax.axis_index("harm") * local_harm + jnp.arange(local_harm, dtype=jnp.int32) + 1
    ).astype(jnp.float32)
    place = lax.axis_index("rows")
    down = RADIX * jnp.arange(SUB, dtype=jnp.int32)[None, :] + jnp.arange(
        RADIX, dtype=jnp.int32
    )[:, None]
    across = (
        RADIX * (lax.rem(place, 2) * HALF + jnp.arange(HALF, dtype=jnp.int32)) + place // 2
    )
    real, imag = propagator(
        (3.0 / H * orders)[:, None, None, None],
        squared_freq_at(down, N)[None, :, None, :],
        squared_freq_at(across, N)[None, None, :, None],
        float(DZ),
    )
    return jnp.stack([real, imag]) * (1.0 / (N * N))


def screen_tables(contrast, absorption):
    orders = jnp.arange(1, H + 1, dtype=jnp.int32).astype(jnp.float32)[:, None, None]
    damping = jnp.exp(-absorption[None] * jnp.power(orders, 1.1) * float(DZ))
    angle = 3.0 / H * orders * float(DZ) * contrast[None]
    return jnp.stack([damping * jnp.cos(angle), damping * jnp.sin(angle)])


def make_constants():
    return tuple(jnp.asarray(table) for table in lane_matrices() + (lane_twiddles(),))


def shards(pressure, contrast, absorption, nonlinearity):
    local_harm = pressure.shape[0]
    constants = make_constants()
    axes = ("harm", "rows")
    pixel_rows = 8
    row_start = lax.axis_index("harm") * pixel_rows

    def own_rows(values):
        return lax.dynamic_slice_in_dim(values, row_start, pixel_rows, 0)

    gain = own_rows(nonlinearity) * (1.0 / (H * math.sqrt(H)))
    gain = gain.reshape(pixel_rows, RADIX, SUB).transpose(1, 0, 2)
    prop = propagator_tables(local_harm)
    screen = screen_tables(own_rows(contrast), own_rows(absorption))

    lines = first_transform(pressure, constants)
    lines = lax.all_to_all(lines, "rows", 0, 0, tiled=True)
    for plane_index in range(PLANES):
        marched = march(lines, prop, (screen, gain), constants, plane_index == 0)
        shape = marched.shape
        marched = lax.all_to_all(marched.reshape((128,) + shape[2:]), axes, 0, 0, tiled=True)
        last = plane_index == PLANES - 1
        lines = pixels(marched.reshape(shape), screen, gain, constants, last)
        if not last:
            lines = lax.all_to_all(lines.reshape((128,) + shape[2:]), axes, 0, 0, tiled=True)
            lines = lines.reshape(shape)
    out = lines.reshape(8, local_harm, pixel_rows * 16, SUB)
    out = lax.all_to_all(out, "harm", 0, 0, tiled=True)
    out = order_rows(out).reshape(local_harm, 8 * pixel_rows, RADIX, 2, SUB)
    return out.transpose(0, 1, 3, 2, 4).reshape(local_harm, 8 * pixel_rows, 2, N)


def solution(mesh):
    in_specs = (P("harm", "rows", None, None), P("rows", None), P("rows", None), P("rows", None))
    out_specs = P("harm", "rows", None, None)
    return jax.shard_map(shards, mesh=mesh, in_specs=in_specs, out_specs=out_specs, check_vma=False)
```

```python
import functools
import math

import jax
import jax.numpy as jnp
import ml_dtypes
import numpy as np
from jax import lax
from jax.experimental import pallas as pl
from jax.experimental.pallas import tpu as pltpu
from jax.sharding import PartitionSpec as P

H = 24
N = 1024
PLANES = 2
DZ = 128
RADIX = 8
SUB = N // RADIX
HALF = SUB // 2
ROOT_HALF = math.sqrt(0.5)
VMEM_LIMIT = 20 * 1024 * 1024


def split_constant(table):
    high = table.astype(np.float32).astype(ml_dtypes.bfloat16)
    low = (table - high.astype(np.float64)).astype(np.float32).astype(ml_dtypes.bfloat16)
    return high, low


def stack_constant(table):
    high, low = split_constant(table)
    return np.concatenate([high, high, low], 0)


def sub_angles():
    index = np.arange(SUB)
    return 2.0 * np.pi / SUB * ((index[:, None] * index[None, :]) % SUB)


def lane_matrices():
    cosine, sine = np.cos(sub_angles()), np.sin(sub_angles())
    forward = np.block([[cosine, -sine], [sine, cosine]])
    inverse = np.block([[cosine, sine], [-sine, cosine]])
    order = np.arange(2 * SUB).reshape(2, 2, HALF).transpose(1, 0, 2).reshape(-1)
    tables = (forward, inverse, forward[:, order], inverse[order])
    return tuple(stack_constant(table) for table in tables)


def lane_twiddles():
    angle = 2.0 * np.pi / N * (np.arange(RADIX)[:, None] * np.arange(SUB)[None, :])
    return np.stack([np.cos(angle), np.sin(angle)]).astype(np.float32)


def split_value(value):
    high = value.astype(jnp.bfloat16)
    low = (value - high.astype(jnp.float32)).astype(jnp.bfloat16)
    return high, low


def add(left, right):
    return tuple(a + b for a, b in zip(left, right))


def subtract(left, right):
    return tuple(a - b for a, b in zip(left, right))


def scale(value, factor):
    return tuple(a * factor for a in value)


def turn_pair(direction):
    def turn(value):
        real, imag = value
        return (imag, -real) if direction < 0 else (-imag, real)

    return turn


def butterflies(points, turn):
    even = [add(points[k], points[k + 4]) for k in range(4)]
    odd = [subtract(points[k], points[k + 4]) for k in range(4)]
    turned = turn(odd[1])
    first = scale(add(odd[1], turned), ROOT_HALF)
    second = turn(odd[2])
    turned = turn(odd[3])
    third = scale(subtract(turned, odd[3]), ROOT_HALF)
    out = [None] * RADIX
    for offset, (a, b, c, d) in ((0, even), (1, (odd[0], first, second, third))):
        sum_ac, diff_ac = add(a, c), subtract(a, c)
        sum_bd, diff_bd = add(b, d), turn(subtract(b, d))
        out[offset] = add(sum_ac, sum_bd)
        out[offset + 4] = subtract(sum_ac, sum_bd)
        out[offset + 2] = add(diff_ac, diff_bd)
        out[offset + 6] = subtract(diff_ac, diff_bd)
    return out


def product(left, right):
    return jnp.dot(left, right, preferred_element_type=jnp.float32)


def store_parts(part_ref, rows, value):
    high, low = split_value(value)
    part_ref[rows, :256] = high
    part_ref[rows, 256:512] = low
    part_ref[rows, 512:] = high


def twiddle_pair(value, cosine, sine, direction):
    real, imag = value
    if direction < 0:
        return real * cosine + imag * sine, imag * cosine - real * sine
    return real * cosine - imag * sine, imag * cosine + real * sine


def fetch(sources, targets, sems):
    copies = [
        pltpu.make_async_copy(source, target, sems.at[index])
        for index, (source, target) in enumerate(zip(sources, targets))
    ]
    for copy in copies:
        copy.start()
    return copies


def forward_lanes(points, store, twiddle_ref):
    for m, value in enumerate(butterflies(points, turn_pair(-1))):
        if m > 0:
            value = twiddle_pair(value, twiddle_ref[0, m : m + 1], twiddle_ref[1, m : m + 1], -1)
        store(m, jnp.concatenate(value, axis=1))


def first_kernel(
    in_ref,
    g_hbm,
    twiddle_hbm,
    out_hbm,
    line_ref,
    part_ref,
    result_ref,
    g_ref,
    twiddle_ref,
    sems,
    out_sems,
):
    local_harm, rows = line_ref.shape[0], result_ref.shape[2]
    lines = rows * 2 * RADIX
    sources = [in_ref.at[pl.ds(n * lines, lines)] for n in range(local_harm)]
    targets = [line_ref.at[n] for n in range(local_harm)]
    twiddle_copy, *copies = fetch(
        [twiddle_hbm, sources[0], g_hbm] + sources[1:],
        [twiddle_ref, targets[0], g_ref] + targets[1:],
        sems,
    )
    g_copy = copies.pop(1)
    twiddle_copy.wait()
    out_copies = []
    for n in range(local_harm):
        copies[n].wait()
        for start in range(0, rows, 16):
            points = [
                tuple(
                    line_ref[n, pl.ds(start * 16 + 2 * k + c, 16, stride=16), :]
                    for c in range(2)
                )
                for k in range(RADIX)
            ]

            def store(m, value):
                first = m * rows + start
                store_parts(part_ref.at[n], slice(first, first + 16), value)

            forward_lanes(points, store, twiddle_ref)
        if n == 0:
            g_copy.wait()
        result = product(part_ref[n], g_ref[...])
        for m in range(RADIX):
            for half in range(2):
                result_ref[n, 2 * m + half] = result[
                    rows * m : rows * m + rows, SUB * half : SUB * half + SUB
                ]
        copy = pltpu.make_async_copy(result_ref.at[n], out_hbm.at[:, n], out_sems.at[n])
        copy.start()
        out_copies.append(copy)
    for copy in out_copies:
        copy.wait()


IN_VMEM = pl.BlockSpec(memory_space=pltpu.VMEM)
IN_HBM = pl.BlockSpec(memory_space=pltpu.HBM)


def in_vmem(*arrays):
    return [pltpu.with_memory_space_constraint(array, pltpu.VMEM) for array in arrays]


def in_hbm(*arrays):
    return [pltpu.with_memory_space_constraint(array, pltpu.HBM) for array in arrays]


def first_transform(pressure, constants):
    local_harm, rows = pressure.shape[0], pressure.shape[1]
    lines = pressure.reshape(local_harm, rows, 2, RADIX, SUB).transpose(0, 1, 3, 2, 4)
    lines = lines.reshape(local_harm * rows * 16, SUB)
    _, _, forward, _, twiddles = constants
    return pl.pallas_call(
        first_kernel,
        in_specs=[IN_HBM] * 3,
        out_specs=IN_HBM,
        out_shape=jax.ShapeDtypeStruct((16, local_harm, rows, SUB), jnp.float32),
        scratch_shapes=[
            pltpu.VMEM((local_harm, rows * 16, SUB), jnp.float32),
            pltpu.VMEM((local_harm, RADIX * rows, 768), jnp.bfloat16),
            pltpu.VMEM((local_harm, 16, rows, SUB), jnp.float32),
            pltpu.VMEM(forward.shape, forward.dtype),
            pltpu.VMEM(twiddles.shape, twiddles.dtype),
            pltpu.SemaphoreType.DMA((local_harm + 2,)),
            pltpu.SemaphoreType.DMA((local_harm,)),
        ],
        compiler_params=pltpu.CompilerParams(vmem_limit_bytes=VMEM_LIMIT),
        cost_estimate=pl.CostEstimate(
            flops=3 * 2 * local_harm * rows * RADIX * 65536,
            bytes_accessed=2 * lines.size * 4,
            transcendentals=0,
        ),
        name="first_transform",
    )(*in_hbm(lines, forward, twiddles))


def march_fetching(in_ref, twiddle_ref, forward_ref, inverse_hbm, prop_ref, *refs):
    inverse_ref, sem = refs[-2:]
    copy = pltpu.make_async_copy(inverse_hbm, inverse_ref, sem)
    copy.start()
    march_kernel(
        True, copy.wait, in_ref, twiddle_ref, forward_ref, inverse_ref, prop_ref, *refs[:-2]
    )


def march_kernel(
    by_rows, wait, in_ref, twiddle_ref, forward_ref, inverse_ref, prop_ref, *refs
):
    out_ref, line_ref, part_ref, spec_ref, back_ref = refs[-5:]
    local_harm = out_ref.shape[2]

    def load(n, block):
        if by_rows:
            return [in_ref[block, n]]
        return [in_ref[tile, block, n] for tile in range(8)]

    part = HALF // 2
    middle = RADIX * local_harm * part
    halves = [slice(half * middle, (half + 1) * middle) for half in range(2)]

    def rows_of(m, n, start, count):
        half, start = divmod(start, part)
        first = half * middle + (m * local_harm + n) * part + start
        return slice(first, first + count)

    def starts(half, count):
        return range(half * part, (half + 1) * part, count)

    def spread(half):
        for n in range(local_harm):
            for start in starts(half, 16):
                points = [
                    tuple(
                        line_ref[n, k, HALF * c + start : HALF * c + start + 16]
                        for c in range(2)
                    )
                    for k in range(RADIX)
                ]
                forward_lanes(
                    points,
                    lambda m, value: store_parts(part_ref, rows_of(m, n, start, 16), value),
                    twiddle_ref,
                )

    def propagate(half):
        for m in range(RADIX):
            for n in range(local_harm):
                for start in starts(half, 16):
                    rows = rows_of(m, n, start, 16)
                    tile = slice(start, start + 16)
                    real, imag = spec_ref[rows, :SUB], spec_ref[rows, SUB:]
                    prop_real, prop_imag = prop_ref[0, n, m, tile], prop_ref[1, n, m, tile]
                    value = (
                        real * prop_real - imag * prop_imag,
                        real * prop_imag + imag * prop_real,
                    )
                    store_parts(part_ref, rows, jnp.concatenate(value, 1))

    def gather(half, n):
        for start in starts(half, 8):
            points = []
            for m in range(RADIX):
                rows = rows_of(m, n, start, 8)
                value = (back_ref[rows, :SUB], back_ref[rows, SUB:])
                if m > 0:
                    value = twiddle_pair(
                        value, twiddle_ref[0, m : m + 1], twiddle_ref[1, m : m + 1], 1
                    )
                points.append(value)
            for k, value in enumerate(butterflies(points, turn_pair(1))):
                for c in range(2):
                    line_ref[n, k, HALF * c + start : HALF * c + start + 8] = value[c]

    for n in range(local_harm):
        for k in range(RADIX):
            columns = jnp.concatenate(load(n, 2 * k) + load(n, 2 * k + 1), 0)
            line_ref[n, k] = columns.T
    first, second = halves
    spread(0)
    spec_ref[first] = product(part_ref[first], forward_ref[...])
    spread(1)
    spec_ref[second] = product(part_ref[second], forward_ref[...])
    wait()
    propagate(0)
    back_ref[first] = product(part_ref[first], inverse_ref[...])
    propagate(1)
    back_ref[second] = product(part_ref[second], inverse_ref[...])
    for n in range(local_harm):
        gather(0, n)
    for n in range(local_harm):
        gather(1, n)
        for k in range(RADIX):
            columns = line_ref[n, k].T
            for tile in range(16):
                out_ref[tile % 8, 2 * k + tile // 8, n] = columns[8 * tile : 8 * tile + 8]


def bring_kernel(*refs):
    count = 2
    for copy in fetch(refs[:count], refs[-count - 1 : -1], refs[-1]):
        copy.wait()


def bring(arrays, after):
    operands = in_hbm(*arrays) + list(after)
    return pl.pallas_call(
        bring_kernel,
        in_specs=[IN_HBM] * len(arrays) + [pl.BlockSpec(memory_space=pl.ANY)] * len(after),
        out_specs=[IN_VMEM] * len(arrays),
        out_shape=[pltpu.VMEM(array.shape, array.dtype) for array in arrays],
        scratch_shapes=[pltpu.SemaphoreType.DMA((len(arrays),))],
        name="bring",
    )(*operands)


def march(wavefield, prop, after, constants, by_rows):
    local_harm = wavefield.shape[1 if by_rows else 2]
    forward, inverse, _, _, twiddles = constants
    kernel = functools.partial(march_kernel, False, lambda: None)
    operands = in_vmem(wavefield, twiddles, forward, inverse, prop)
    in_specs = [IN_VMEM] * len(operands)
    if by_rows:
        kernel = march_fetching
        operands[1:3] = in_vmem(*bring([twiddles, forward], after[:1]))
        operands[3:4] = in_hbm(inverse)
        operands += in_hbm(*after)
        in_specs[3] = IN_HBM
        in_specs += [IN_HBM] * len(after)
    scratch = [
        pltpu.VMEM((local_harm, RADIX, SUB, SUB), jnp.float32),
        pltpu.VMEM((RADIX * local_harm * HALF, 768), jnp.bfloat16),
        pltpu.VMEM((RADIX * local_harm * HALF, 2 * SUB), jnp.float32),
        pltpu.VMEM((RADIX * local_harm * HALF, 2 * SUB), jnp.float32),
    ]
    if by_rows:
        scratch += [pltpu.VMEM(inverse.shape, inverse.dtype), pltpu.SemaphoreType.DMA]
    return pl.pallas_call(
        kernel,
        in_specs=in_specs,
        out_specs=IN_VMEM,
        out_shape=pltpu.VMEM((8, 16, local_harm, 8, SUB), jnp.float32),
        scratch_shapes=scratch,
        compiler_params=pltpu.CompilerParams(vmem_limit_bytes=VMEM_LIMIT),
        cost_estimate=pl.CostEstimate(
            flops=2 * 2 * local_harm * 512 * 768 * 256,
            bytes_accessed=4 * wavefield.size * 4,
            transcendentals=0,
        ),
        name="march",
    )(*operands)


class Network:
    def __init__(self, inputs):
        self.inputs = inputs
        self.terms = [()] * inputs
        self.known = {}

    def node(self, terms):
        if terms not in self.known:
            self.known[terms] = len(self.terms)
            self.terms.append(terms)
        return self.known[terms]

    def negate(self, x):
        return None if x is None else (-x[0], x[1])

    def scale(self, factor, x):
        if x is None:
            return None
        sign = x[0] if factor > 0 else -x[0]
        return (sign, self.node(((abs(factor), x[1]),)))

    def add(self, x, y):
        if x is None or y is None:
            return y if x is None else x
        if x[1] > y[1]:
            x, y = y, x
        return (x[0], self.node(((1.0, x[1]), (float(x[0] * y[0]), y[1]))))

    def subtract(self, x, y):
        return self.add(x, self.negate(y))

    def rotate(self, turns, z):
        cosine, sine = math.cos(2.0 * math.pi * turns), math.sin(2.0 * math.pi * turns)
        real, imag = z
        if turns == 0.0:
            return z
        if turns == 0.25:
            return (self.negate(imag), real)
        if turns == 0.125:
            return (
                self.scale(cosine, self.subtract(real, imag)),
                self.scale(cosine, self.add(imag, real)),
            )
        return (
            self.subtract(self.scale(cosine, real), self.scale(sine, imag)),
            self.add(self.scale(cosine, imag), self.scale(sine, real)),
        )

    def five_points(self, x):
        def both(operation, a, b):
            return (operation(a[0], b[0]), operation(a[1], b[1]))

        def times(factor, a):
            return (self.scale(factor, a[0]), self.scale(factor, a[1]))

        def turned(a):
            return (self.negate(a[1]), a[0])

        plus, minus = self.add, self.subtract
        sum_1, sum_2 = both(plus, x[1], x[4]), both(plus, x[2], x[3])
        diff_1, diff_2 = both(minus, x[1], x[4]), both(minus, x[2], x[3])
        total, gap = both(plus, sum_1, sum_2), both(minus, sum_1, sum_2)
        base, step = both(plus, x[0], times(-0.25, total)), times(math.sqrt(5.0) / 4.0, gap)
        even_1, even_2 = both(plus, base, step), both(minus, base, step)
        sine_1, sine_2 = math.sin(0.4 * math.pi), math.sin(0.8 * math.pi)
        odd_1 = turned(both(plus, times(sine_1, diff_1), times(sine_2, diff_2)))
        odd_2 = turned(both(minus, times(sine_2, diff_1), times(sine_1, diff_2)))
        return [
            both(plus, x[0], total),
            both(plus, even_1, odd_1),
            both(plus, even_2, odd_2),
            both(minus, even_2, odd_2),
            both(minus, even_1, odd_1),
        ]

    def real_points(self, u, length):
        if length == 1:
            return [u[0][0]]
        half = length // 2
        out = [None] * length
        for odd in range(2):
            folded = {}
            for k, z in u.items():
                z = self.rotate(k * odd / length, z)
                k %= half
                if 2 * k > half:
                    k, z = half - k, (z[0], self.negate(z[1]))
                old = folded.get(k, (None, None))
                folded[k] = (self.add(old[0], z[0]), self.add(old[1], z[1]))
            for k in folded:
                if k == 0 or 2 * k == half:
                    folded[k] = (folded[k][0], None)
            out[odd::2] = self.real_points(folded, half)
        return out


def sample_network():
    assert 3 * H < 80
    network = Network(2 * H)
    grid = [[(None, None)] * 5 for _ in range(9)]
    for n in range(1, H + 1):
        real, imag = (1, 2 * n - 2), (1, 2 * n - 1)
        k, place = n % 16, n % 5
        if k > 8:
            k, place, imag = 16 - k, -n % 5, network.negate(imag)
        grid[k][place] = (real, imag)
    columns = [network.five_points(row) for row in grid]
    groups = []
    for instant in range(5):
        start = len(network.terms)
        u = {k: columns[k][instant] for k in range(9)}
        u[0], u[8] = (u[0][0], None), (u[8][0], None)
        groups.append((start, network.real_points(u, 16)))
    return network, groups


def signed_sum(old, sign, value):
    if old is None:
        return (sign, value)
    if old[0] == sign:
        return (sign, old[1] + value)
    return (1, old[1] - value) if old[0] > 0 else (1, value - old[1])


def couple_pixels(load, gain, store):
    network, groups = sample_network()
    values = {}

    def value(node):
        if node not in values:
            if node < network.inputs:
                values[node] = load(node)
            else:
                terms = network.terms[node]
                first = value(terms[0][1])
                if len(terms) == 1:
                    values[node] = terms[0][0] * first
                else:
                    second = value(terms[1][1])
                    values[node] = first + second if terms[1][0] > 0 else first - second
        return values[node]

    sums = [None] * len(network.terms)
    end = len(network.terms)
    for start, outputs in reversed([(network.inputs, [])] + groups):
        for sign, node in outputs:
            sample = value(node)
            sums[node] = signed_sum(sums[node], sign, sample * sample)
        for node in range(end - 1, start - 1, -1):
            if sums[node] is None:
                continue
            sign, total = sums[node]
            for factor, source in network.terms[node]:
                if abs(factor) == 1.0:
                    part = (sign if factor > 0 else -sign, total)
                else:
                    part = (sign, factor * total)
                sums[source] = signed_sum(sums[source], *part)
        end = start
    for n in range(1, H + 1):
        weight = (n * 4.0 / 80.0) * gain
        (sign_real, real), (sign_imag, imag) = sums[2 * n - 2], sums[2 * n - 1]
        old_real, old_imag = load(2 * n - 2), load(2 * n - 1)
        turn_real, turn_imag = weight * imag, weight * real
        store(
            n,
            old_real - turn_real if sign_imag > 0 else old_real + turn_real,
            old_imag + turn_imag if sign_real > 0 else old_imag - turn_imag,
        )


def pixel_kernel(
    last,
    in_ref,
    inverse_ref,
    twiddle_ref,
    screen_ref,
    gain_ref,
    forward_ref,
    out_ref,
    part_ref,
    line_ref,
    field_ref,
):
    local_harm = H // 8
    part = H // 2
    height = 8 * part
    middle = RADIX * height
    halves = [slice(half * middle, (half + 1) * middle) for half in range(2)]

    def orders(half, step):
        return range(half * part, (half + 1) * part, step)

    def rows_of(block, n, count):
        half, n = divmod(n, part)
        first = half * middle + height * block + 8 * n
        return slice(first, first + count)

    def tile_of(n, r):
        return in_ref[n // local_harm, r, n % local_harm]

    def split_half(half):
        for n in orders(half, 2):
            for m in range(RADIX):
                value = jnp.concatenate(
                    [
                        jnp.concatenate([tile_of(n + i, 2 * m), tile_of(n + i, 2 * m + 1)], 1)
                        for i in range(2)
                    ],
                    0,
                )
                store_parts(part_ref, rows_of(m, n, 16), value)

    def screen_half(half):
        for n in orders(half, 1):
            points = []
            for m in range(RADIX):
                rows = rows_of(m, n, 8)
                value = (line_ref[rows, :SUB], line_ref[rows, SUB:])
                if m > 0:
                    value = twiddle_pair(
                        value, twiddle_ref[0, m : m + 1], twiddle_ref[1, m : m + 1], 1
                    )
                points.append(value)
            for k, (real, imag) in enumerate(butterflies(points, turn_pair(1))):
                lanes = slice(SUB * k, SUB * k + SUB)
                factor_real, factor_imag = screen_ref[0, n, :, lanes], screen_ref[1, n, :, lanes]
                field_ref[k, 2 * n] = real * factor_real - imag * factor_imag
                field_ref[k, 2 * n + 1] = real * factor_imag + imag * factor_real

    first, second = halves
    split_half(0)
    line_ref[first] = product(part_ref[first], inverse_ref[...])
    split_half(1)
    line_ref[second] = product(part_ref[second], inverse_ref[...])
    screen_half(0)
    screen_half(1)

    def one_block(k, carry):
        def load(index):
            return field_ref[k, index]

        def store(n, real, imag):
            if last:
                start = 128 * (n - 1) + 2 * k
                out_ref[pl.ds(start, 8, stride=16), :] = real
                out_ref[pl.ds(start + 1, 8, stride=16), :] = imag
            else:
                field_ref[k, 2 * n - 2] = real
                field_ref[k, 2 * n - 1] = imag

        couple_pixels(load, gain_ref[k], store)
        return carry

    lax.fori_loop(0, RADIX, one_block, 0)
    if last:
        return

    def spread_half(half):
        for n in orders(half, 2):
            points = [
                tuple(
                    jnp.concatenate([field_ref[k, 2 * n + c], field_ref[k, 2 * n + 2 + c]], 0)
                    for c in range(2)
                )
                for k in range(RADIX)
            ]
            forward_lanes(
                points,
                lambda m, value: store_parts(part_ref, rows_of(m, n, 16), value),
                twiddle_ref,
            )

    def store_half(half):
        result = product(part_ref[halves[half]], forward_ref[...])
        for m in range(RADIX):
            for n in orders(half, 1):
                row = height * m + 8 * (n - half * part)
                for side in range(2):
                    out_ref[n // local_harm, 2 * m + side, n % local_harm] = result[
                        row : row + 8, SUB * side : SUB * side + SUB
                    ]

    spread_half(0)
    store_half(0)
    spread_half(1)
    store_half(1)


def pixels(wavefield, screen, gain, constants, last):
    _, _, forward, inverse, twiddles = constants
    tables = [inverse, twiddles, screen, gain, forward]
    operands = in_vmem(wavefield, *tables)
    out_shape = (H * 8 * 16, SUB) if last else wavefield.shape
    return pl.pallas_call(
        functools.partial(pixel_kernel, last),
        in_specs=[IN_VMEM] * len(operands),
        out_specs=IN_VMEM,
        out_shape=pltpu.VMEM(out_shape, jnp.float32),
        scratch_shapes=[
            pltpu.VMEM((RADIX * 8 * H, 768), jnp.bfloat16),
            pltpu.VMEM((RADIX * 8 * H, 2 * SUB), jnp.float32),
            pltpu.VMEM((RADIX, 2 * H, 8, SUB), jnp.float32),
        ],
        compiler_params=pltpu.CompilerParams(vmem_limit_bytes=VMEM_LIMIT),
        cost_estimate=pl.CostEstimate(
            flops=2 * 3 * 2 * 8 * H * RADIX * 65536,
            bytes_accessed=4 * wavefield.size * 4,
            transcendentals=0,
        ),
        name="pixels_last" if last else "pixels",
    )(*operands)


def order_kernel(in_ref, out_ref, sems):
    orders = range(in_ref.shape[1])
    copies = fetch([in_ref.at[:, n] for n in orders], [out_ref.at[n] for n in orders], sems)
    for copy in copies:
        copy.wait()


def order_rows(blocks):
    groups, local_harm = blocks.shape[:2]
    return pl.pallas_call(
        order_kernel,
        in_specs=[IN_VMEM],
        out_specs=IN_HBM,
        out_shape=jax.ShapeDtypeStruct((local_harm, groups) + blocks.shape[2:], blocks.dtype),
        scratch_shapes=[pltpu.SemaphoreType.DMA((local_harm,))],
        name="order_rows",
    )(*in_vmem(blocks))


def squared_freq_at(indices, length):
    centred = jnp.where(indices < length // 2, indices, indices - length).astype(jnp.float32)
    scaled = centred * (2.0 * math.pi / length)
    return scaled * scaled


def propagator(wave_number, down_square, across_square, march_step):
    axial_square = wave_number * wave_number - down_square - across_square
    axial_root = jnp.sqrt(jnp.abs(axial_square))
    phase_turn = march_step * axial_root
    propagating = axial_square >= 0.0
    prop_real = jnp.where(propagating, jnp.cos(phase_turn), jnp.exp(-phase_turn))
    prop_imag = jnp.where(propagating, jnp.sin(phase_turn), 0.0)
    return (prop_real, prop_imag)


def propagator_tables(local_harm):
    orders = (
        lax.axis_index("harm") * local_harm + jnp.arange(local_harm, dtype=jnp.int32) + 1
    ).astype(jnp.float32)
    place = lax.axis_index("rows")
    down = RADIX * jnp.arange(SUB, dtype=jnp.int32)[None, :] + jnp.arange(
        RADIX, dtype=jnp.int32
    )[:, None]
    across = (
        RADIX * (lax.rem(place, 2) * HALF + jnp.arange(HALF, dtype=jnp.int32)) + place // 2
    )
    real, imag = propagator(
        (3.0 / H * orders)[:, None, None, None],
        squared_freq_at(down, N)[None, :, None, :],
        squared_freq_at(across, N)[None, None, :, None],
        float(DZ),
    )
    return jnp.stack([real, imag]) * (1.0 / (N * N))


def screen_tables(contrast, absorption):
    orders = jnp.arange(1, H + 1, dtype=jnp.int32).astype(jnp.float32)[:, None, None]
    damping = jnp.exp(-absorption[None] * jnp.power(orders, 1.1) * float(DZ))
    angle = 3.0 / H * orders * float(DZ) * contrast[None]
    return jnp.stack([damping * jnp.cos(angle), damping * jnp.sin(angle)])


def make_constants():
    return tuple(jnp.asarray(table) for table in lane_matrices() + (lane_twiddles(),))


def shards(pressure, contrast, absorption, nonlinearity):
    local_harm = pressure.shape[0]
    constants = make_constants()
    axes = ("harm", "rows")
    pixel_rows = 8
    row_start = lax.axis_index("harm") * pixel_rows

    def own_rows(values):
        return lax.dynamic_slice_in_dim(values, row_start, pixel_rows, 0)

    gain = own_rows(nonlinearity) * (1.0 / (H * math.sqrt(H)))
    gain = gain.reshape(pixel_rows, RADIX, SUB).transpose(1, 0, 2)
    prop = propagator_tables(local_harm)
    screen = screen_tables(own_rows(contrast), own_rows(absorption))

    lines = first_transform(pressure, constants)
    lines = lax.all_to_all(lines, "rows", 0, 0, tiled=True)
    for plane_index in range(PLANES):
        marched = march(lines, prop, (screen, gain), constants, plane_index == 0)
        shape = marched.shape
        marched = lax.all_to_all(marched.reshape((128,) + shape[2:]), axes, 0, 0, tiled=True)
        last = plane_index == PLANES - 1
        lines = pixels(marched.reshape(shape), screen, gain, constants, last)
        if not last:
            lines = lax.all_to_all(lines.reshape((128,) + shape[2:]), axes, 0, 0, tiled=True)
            lines = lines.reshape(shape)
    out = lines.reshape(8, local_harm, pixel_rows * 16, SUB)
    out = lax.all_to_all(out, "harm", 0, 0, tiled=True)
    out = order_rows(out).reshape(local_harm, 8 * pixel_rows, RADIX, 2, SUB)
    return out.transpose(0, 1, 3, 2, 4).reshape(local_harm, 8 * pixel_rows, 2, N)


def solution(mesh):
    in_specs = (P("harm", "rows", None, None), P("rows", None), P("rows", None), P("rows", None))
    out_specs = P("harm", "rows", None, None)
    return jax.shard_map(shards, mesh=mesh, in_specs=in_specs, out_specs=out_specs, check_vma=False)
```

```python
import functools
import math

import jax
import jax.numpy as jnp
import ml_dtypes
import numpy as np
from jax import lax
from jax.experimental import pallas as pl
from jax.experimental.pallas import tpu as pltpu
from jax.sharding import PartitionSpec as P

H = 24
N = 1024
PLANES = 2
DZ = 128
RADIX = 8
SUB = N // RADIX
HALF = SUB // 2
ROOT_HALF = math.sqrt(0.5)
VMEM_LIMIT = 20 * 1024 * 1024


def split_constant(table):
    high = table.astype(np.float32).astype(ml_dtypes.bfloat16)
    low = (table - high.astype(np.float64)).astype(np.float32).astype(ml_dtypes.bfloat16)
    return high, low


def stack_constant(table):
    high, low = split_constant(table)
    return np.concatenate([high, high, low], 0)


def sub_angles():
    index = np.arange(SUB)
    return 2.0 * np.pi / SUB * ((index[:, None] * index[None, :]) % SUB)


def lane_matrices():
    cosine, sine = np.cos(sub_angles()), np.sin(sub_angles())
    forward = np.block([[cosine, -sine], [sine, cosine]])
    inverse = np.block([[cosine, sine], [-sine, cosine]])
    order = np.arange(2 * SUB).reshape(2, 2, HALF).transpose(1, 0, 2).reshape(-1)
    tables = (forward, inverse, forward[:, order], inverse[order])
    return tuple(stack_constant(table) for table in tables)


def lane_twiddles():
    angle = 2.0 * np.pi / N * (np.arange(RADIX)[:, None] * np.arange(SUB)[None, :])
    return np.stack([np.cos(angle), np.sin(angle)]).astype(np.float32)


def split_value(value):
    high = value.astype(jnp.bfloat16)
    low = (value - high.astype(jnp.float32)).astype(jnp.bfloat16)
    return high, low


def add(left, right):
    return tuple(a + b for a, b in zip(left, right))


def subtract(left, right):
    return tuple(a - b for a, b in zip(left, right))


def scale(value, factor):
    return tuple(a * factor for a in value)


def turn_pair(direction):
    def turn(value):
        real, imag = value
        return (imag, -real) if direction < 0 else (-imag, real)

    return turn


def butterflies(points, turn):
    even = [add(points[k], points[k + 4]) for k in range(4)]
    odd = [subtract(points[k], points[k + 4]) for k in range(4)]
    turned = turn(odd[1])
    first = scale(add(odd[1], turned), ROOT_HALF)
    second = turn(odd[2])
    turned = turn(odd[3])
    third = scale(subtract(turned, odd[3]), ROOT_HALF)
    out = [None] * RADIX
    for offset, (a, b, c, d) in ((0, even), (1, (odd[0], first, second, third))):
        sum_ac, diff_ac = add(a, c), subtract(a, c)
        sum_bd, diff_bd = add(b, d), turn(subtract(b, d))
        out[offset] = add(sum_ac, sum_bd)
        out[offset + 4] = subtract(sum_ac, sum_bd)
        out[offset + 2] = add(diff_ac, diff_bd)
        out[offset + 6] = subtract(diff_ac, diff_bd)
    return out


def product(left, right):
    return jnp.dot(left, right, preferred_element_type=jnp.float32)


def store_parts(part_ref, rows, value):
    high, low = split_value(value)
    part_ref[rows, :256] = high
    part_ref[rows, 256:512] = low
    part_ref[rows, 512:] = high


def twiddle_pair(value, cosine, sine, direction):
    real, imag = value
    if direction < 0:
        return real * cosine + imag * sine, imag * cosine - real * sine
    return real * cosine - imag * sine, imag * cosine + real * sine


def fetch(sources, targets, sems):
    copies = [
        pltpu.make_async_copy(source, target, sems.at[index])
        for index, (source, target) in enumerate(zip(sources, targets))
    ]
    for copy in copies:
        copy.start()
    return copies


def forward_lanes(points, store, twiddle_ref):
    for m, value in enumerate(butterflies(points, turn_pair(-1))):
        if m > 0:
            value = twiddle_pair(value, twiddle_ref[0, m : m + 1], twiddle_ref[1, m : m + 1], -1)
        store(m, jnp.concatenate(value, axis=1))


def first_kernel(
    in_ref,
    g_hbm,
    twiddle_hbm,
    out_hbm,
    line_ref,
    part_ref,
    result_ref,
    g_ref,
    twiddle_ref,
    sems,
    out_sems,
):
    local_harm, rows = line_ref.shape[0], result_ref.shape[2]
    lines = rows * 2 * RADIX
    pieces = [(n, start) for n in range(local_harm) for start in range(0, lines, 256)]
    sources = [in_ref.at[pl.ds(n * lines + start, 256)] for n, start in pieces]
    targets = [line_ref.at[n, pl.ds(start, 256)] for n, start in pieces]
    twiddle_copy, *copies = fetch(
        [twiddle_hbm, sources[0], g_hbm] + sources[1:],
        [twiddle_ref, targets[0], g_ref] + targets[1:],
        sems,
    )
    g_copy = copies.pop(1)
    twiddle_copy.wait()
    out_copies = []
    for n in range(local_harm):
        for start in range(0, rows, 16):
            copies[(n * rows + start) // 16].wait()
            points = [
                tuple(
                    line_ref[n, pl.ds(start * 16 + 2 * k + c, 16, stride=16), :]
                    for c in range(2)
                )
                for k in range(RADIX)
            ]

            def store(m, value):
                first = m * rows + start
                store_parts(part_ref.at[n], slice(first, first + 16), value)

            forward_lanes(points, store, twiddle_ref)
        if n == 0:
            g_copy.wait()
        result = product(part_ref[n], g_ref[...])
        for m in range(RADIX):
            for half in range(2):
                result_ref[n, 2 * m + half] = result[
                    rows * m : rows * m + rows, SUB * half : SUB * half + SUB
                ]
        copy = pltpu.make_async_copy(result_ref.at[n], out_hbm.at[:, n], out_sems.at[n])
        copy.start()
        out_copies.append(copy)
    for copy in out_copies:
        copy.wait()


IN_VMEM = pl.BlockSpec(memory_space=pltpu.VMEM)
IN_HBM = pl.BlockSpec(memory_space=pltpu.HBM)


def in_vmem(*arrays):
    return [pltpu.with_memory_space_constraint(array, pltpu.VMEM) for array in arrays]


def in_hbm(*arrays):
    return [pltpu.with_memory_space_constraint(array, pltpu.HBM) for array in arrays]


def first_transform(pressure, constants):
    local_harm, rows = pressure.shape[0], pressure.shape[1]
    lines = pressure.reshape(local_harm, rows, 2, RADIX, SUB).transpose(0, 1, 3, 2, 4)
    lines = lines.reshape(local_harm * rows * 16, SUB)
    _, _, forward, _, twiddles = constants
    return pl.pallas_call(
        first_kernel,
        in_specs=[IN_HBM] * 3,
        out_specs=IN_HBM,
        out_shape=jax.ShapeDtypeStruct((16, local_harm, rows, SUB), jnp.float32),
        scratch_shapes=[
            pltpu.VMEM((local_harm, rows * 16, SUB), jnp.float32),
            pltpu.VMEM((local_harm, RADIX * rows, 768), jnp.bfloat16),
            pltpu.VMEM((local_harm, 16, rows, SUB), jnp.float32),
            pltpu.VMEM(forward.shape, forward.dtype),
            pltpu.VMEM(twiddles.shape, twiddles.dtype),
            pltpu.SemaphoreType.DMA((local_harm * rows // 16 + 2,)),
            pltpu.SemaphoreType.DMA((local_harm,)),
        ],
        compiler_params=pltpu.CompilerParams(vmem_limit_bytes=VMEM_LIMIT),
        cost_estimate=pl.CostEstimate(
            flops=3 * 2 * local_harm * rows * RADIX * 65536,
            bytes_accessed=2 * lines.size * 4,
            transcendentals=0,
        ),
        name="first_transform",
    )(*in_hbm(lines, forward, twiddles))


def march_fetching(in_ref, twiddle_ref, forward_ref, inverse_hbm, prop_ref, *refs):
    inverse_ref, sem = refs[-2:]
    copy = pltpu.make_async_copy(inverse_hbm, inverse_ref, sem)
    copy.start()
    march_kernel(
        True, copy.wait, in_ref, twiddle_ref, forward_ref, inverse_ref, prop_ref, *refs[:-2]
    )


def march_kernel(
    by_rows, wait, in_ref, twiddle_ref, forward_ref, inverse_ref, prop_ref, *refs
):
    out_ref, line_ref, part_ref, spec_ref, back_ref = refs[-5:]
    local_harm = out_ref.shape[2]

    def load(n, block):
        if by_rows:
            return [in_ref[block, n]]
        return [in_ref[tile, block, n] for tile in range(8)]

    part = HALF // 2
    middle = RADIX * local_harm * part
    halves = [slice(half * middle, (half + 1) * middle) for half in range(2)]

    def rows_of(m, n, start, count):
        half, start = divmod(start, part)
        first = half * middle + (m * local_harm + n) * part + start
        return slice(first, first + count)

    def starts(half, count):
        return range(half * part, (half + 1) * part, count)

    def spread(half):
        for n in range(local_harm):
            for start in starts(half, 16):
                points = [
                    tuple(
                        line_ref[n, k, HALF * c + start : HALF * c + start + 16]
                        for c in range(2)
                    )
                    for k in range(RADIX)
                ]
                forward_lanes(
                    points,
                    lambda m, value: store_parts(part_ref, rows_of(m, n, start, 16), value),
                    twiddle_ref,
                )

    def propagate(half):
        for m in range(RADIX):
            for n in range(local_harm):
                for start in starts(half, 16):
                    rows = rows_of(m, n, start, 16)
                    tile = slice(start, start + 16)
                    real, imag = spec_ref[rows, :SUB], spec_ref[rows, SUB:]
                    prop_real, prop_imag = prop_ref[0, n, m, tile], prop_ref[1, n, m, tile]
                    value = (
                        real * prop_real - imag * prop_imag,
                        real * prop_imag + imag * prop_real,
                    )
                    store_parts(part_ref, rows, jnp.concatenate(value, 1))

    def gather(half, n):
        for start in starts(half, 8):
            points = []
            for m in range(RADIX):
                rows = rows_of(m, n, start, 8)
                value = (back_ref[rows, :SUB], back_ref[rows, SUB:])
                if m > 0:
                    value = twiddle_pair(
                        value, twiddle_ref[0, m : m + 1], twiddle_ref[1, m : m + 1], 1
                    )
                points.append(value)
            for k, value in enumerate(butterflies(points, turn_pair(1))):
                for c in range(2):
                    line_ref[n, k, HALF * c + start : HALF * c + start + 8] = value[c]

    for n in range(local_harm):
        for k in range(RADIX):
            columns = jnp.concatenate(load(n, 2 * k) + load(n, 2 * k + 1), 0)
            line_ref[n, k] = columns.T
    first, second = halves
    spread(0)
    spec_ref[first] = product(part_ref[first], forward_ref[...])
    spread(1)
    spec_ref[second] = product(part_ref[second], forward_ref[...])
    wait()
    propagate(0)
    back_ref[first] = product(part_ref[first], inverse_ref[...])
    propagate(1)
    back_ref[second] = product(part_ref[second], inverse_ref[...])
    for n in range(local_harm):
        gather(0, n)
    for n in range(local_harm):
        gather(1, n)
        for k in range(RADIX):
            columns = line_ref[n, k].T
            for tile in range(16):
                out_ref[tile % 8, 2 * k + tile // 8, n] = columns[8 * tile : 8 * tile + 8]


def bring_kernel(*refs):
    count = 2
    for copy in fetch(refs[:count], refs[-count - 1 : -1], refs[-1]):
        copy.wait()


def bring(arrays, after):
    operands = in_hbm(*arrays) + list(after)
    return pl.pallas_call(
        bring_kernel,
        in_specs=[IN_HBM] * len(arrays) + [pl.BlockSpec(memory_space=pl.ANY)] * len(after),
        out_specs=[IN_VMEM] * len(arrays),
        out_shape=[pltpu.VMEM(array.shape, array.dtype) for array in arrays],
        scratch_shapes=[pltpu.SemaphoreType.DMA((len(arrays),))],
        name="bring",
    )(*operands)


def march(wavefield, prop, after, constants, by_rows):
    local_harm = wavefield.shape[1 if by_rows else 2]
    forward, inverse, _, _, twiddles = constants
    kernel = functools.partial(march_kernel, False, lambda: None)
    operands = in_vmem(wavefield, twiddles, forward, inverse, prop)
    in_specs = [IN_VMEM] * len(operands)
    if by_rows:
        kernel = march_fetching
        operands[1:3] = in_vmem(*bring([twiddles, forward], after[:1]))
        operands[3:4] = in_hbm(inverse)
        operands += in_hbm(*after)
        in_specs[3] = IN_HBM
        in_specs += [IN_HBM] * len(after)
    scratch = [
        pltpu.VMEM((local_harm, RADIX, SUB, SUB), jnp.float32),
        pltpu.VMEM((RADIX * local_harm * HALF, 768), jnp.bfloat16),
        pltpu.VMEM((RADIX * local_harm * HALF, 2 * SUB), jnp.float32),
        pltpu.VMEM((RADIX * local_harm * HALF, 2 * SUB), jnp.float32),
    ]
    if by_rows:
        scratch += [pltpu.VMEM(inverse.shape, inverse.dtype), pltpu.SemaphoreType.DMA]
    return pl.pallas_call(
        kernel,
        in_specs=in_specs,
        out_specs=IN_VMEM,
        out_shape=pltpu.VMEM((8, 16, local_harm, 8, SUB), jnp.float32),
        scratch_shapes=scratch,
        compiler_params=pltpu.CompilerParams(vmem_limit_bytes=VMEM_LIMIT),
        cost_estimate=pl.CostEstimate(
            flops=2 * 2 * local_harm * 512 * 768 * 256,
            bytes_accessed=4 * wavefield.size * 4,
            transcendentals=0,
        ),
        name="march",
    )(*operands)


class Network:
    def __init__(self, inputs):
        self.inputs = inputs
        self.terms = [()] * inputs
        self.known = {}

    def node(self, terms):
        if terms not in self.known:
            self.known[terms] = len(self.terms)
            self.terms.append(terms)
        return self.known[terms]

    def negate(self, x):
        return None if x is None else (-x[0], x[1])

    def scale(self, factor, x):
        if x is None:
            return None
        sign = x[0] if factor > 0 else -x[0]
        return (sign, self.node(((abs(factor), x[1]),)))

    def add(self, x, y):
        if x is None or y is None:
            return y if x is None else x
        if x[1] > y[1]:
            x, y = y, x
        return (x[0], self.node(((1.0, x[1]), (float(x[0] * y[0]), y[1]))))

    def subtract(self, x, y):
        return self.add(x, self.negate(y))

    def rotate(self, turns, z):
        cosine, sine = math.cos(2.0 * math.pi * turns), math.sin(2.0 * math.pi * turns)
        real, imag = z
        if turns == 0.0:
            return z
        if turns == 0.25:
            return (self.negate(imag), real)
        if turns == 0.125:
            return (
                self.scale(cosine, self.subtract(real, imag)),
                self.scale(cosine, self.add(imag, real)),
            )
        return (
            self.subtract(self.scale(cosine, real), self.scale(sine, imag)),
            self.add(self.scale(cosine, imag), self.scale(sine, real)),
        )

    def five_points(self, x):
        def both(operation, a, b):
            return (operation(a[0], b[0]), operation(a[1], b[1]))

        def times(factor, a):
            return (self.scale(factor, a[0]), self.scale(factor, a[1]))

        def turned(a):
            return (self.negate(a[1]), a[0])

        plus, minus = self.add, self.subtract
        sum_1, sum_2 = both(plus, x[1], x[4]), both(plus, x[2], x[3])
        diff_1, diff_2 = both(minus, x[1], x[4]), both(minus, x[2], x[3])
        total, gap = both(plus, sum_1, sum_2), both(minus, sum_1, sum_2)
        base, step = both(plus, x[0], times(-0.25, total)), times(math.sqrt(5.0) / 4.0, gap)
        even_1, even_2 = both(plus, base, step), both(minus, base, step)
        sine_1, sine_2 = math.sin(0.4 * math.pi), math.sin(0.8 * math.pi)
        odd_1 = turned(both(plus, times(sine_1, diff_1), times(sine_2, diff_2)))
        odd_2 = turned(both(minus, times(sine_2, diff_1), times(sine_1, diff_2)))
        return [
            both(plus, x[0], total),
            both(plus, even_1, odd_1),
            both(plus, even_2, odd_2),
            both(minus, even_2, odd_2),
            both(minus, even_1, odd_1),
        ]

    def real_points(self, u, length):
        if length == 1:
            return [u[0][0]]
        half = length // 2
        out = [None] * length
        for odd in range(2):
            folded = {}
            for k, z in u.items():
                z = self.rotate(k * odd / length, z)
                k %= half
                if 2 * k > half:
                    k, z = half - k, (z[0], self.negate(z[1]))
                old = folded.get(k, (None, None))
                folded[k] = (self.add(old[0], z[0]), self.add(old[1], z[1]))
            for k in folded:
                if k == 0 or 2 * k == half:
                    folded[k] = (folded[k][0], None)
            out[odd::2] = self.real_points(folded, half)
        return out


def sample_network():
    assert 3 * H < 80
    network = Network(2 * H)
    grid = [[(None, None)] * 5 for _ in range(9)]
    for n in range(1, H + 1):
        real, imag = (1, 2 * n - 2), (1, 2 * n - 1)
        k, place = n % 16, n % 5
        if k > 8:
            k, place, imag = 16 - k, -n % 5, network.negate(imag)
        grid[k][place] = (real, imag)
    columns = [network.five_points(row) for row in grid]
    groups = []
    for instant in range(5):
        start = len(network.terms)
        u = {k: columns[k][instant] for k in range(9)}
        u[0], u[8] = (u[0][0], None), (u[8][0], None)
        groups.append((start, network.real_points(u, 16)))
    return network, groups


def signed_sum(old, sign, value):
    if old is None:
        return (sign, value)
    if old[0] == sign:
        return (sign, old[1] + value)
    return (1, old[1] - value) if old[0] > 0 else (1, value - old[1])


def couple_pixels(load, gain, store):
    network, groups = sample_network()
    values = {}

    def value(node):
        if node not in values:
            if node < network.inputs:
                values[node] = load(node)
            else:
                terms = network.terms[node]
                first = value(terms[0][1])
                if len(terms) == 1:
                    values[node] = terms[0][0] * first
                else:
                    second = value(terms[1][1])
                    values[node] = first + second if terms[1][0] > 0 else first - second
        return values[node]

    sums = [None] * len(network.terms)
    end = len(network.terms)
    for start, outputs in reversed([(network.inputs, [])] + groups):
        for sign, node in outputs:
            sample = value(node)
            sums[node] = signed_sum(sums[node], sign, sample * sample)
        for node in range(end - 1, start - 1, -1):
            if sums[node] is None:
                continue
            sign, total = sums[node]
            for factor, source in network.terms[node]:
                if abs(factor) == 1.0:
                    part = (sign if factor > 0 else -sign, total)
                else:
                    part = (sign, factor * total)
                sums[source] = signed_sum(sums[source], *part)
        end = start
    for n in range(1, H + 1):
        weight = (n * 4.0 / 80.0) * gain
        (sign_real, real), (sign_imag, imag) = sums[2 * n - 2], sums[2 * n - 1]
        old_real, old_imag = load(2 * n - 2), load(2 * n - 1)
        turn_real, turn_imag = weight * imag, weight * real
        store(
            n,
            old_real - turn_real if sign_imag > 0 else old_real + turn_real,
            old_imag + turn_imag if sign_real > 0 else old_imag - turn_imag,
        )


def pixel_kernel(
    last,
    in_ref,
    inverse_ref,
    twiddle_ref,
    screen_ref,
    gain_ref,
    forward_ref,
    out_ref,
    part_ref,
    line_ref,
    field_ref,
):
    local_harm = H // 8
    part = H // 2
    height = 8 * part
    middle = RADIX * height
    halves = [slice(half * middle, (half + 1) * middle) for half in range(2)]

    def orders(half, step):
        return range(half * part, (half + 1) * part, step)

    def rows_of(block, n, count):
        half, n = divmod(n, part)
        first = half * middle + height * block + 8 * n
        return slice(first, first + count)

    def tile_of(n, r):
        return in_ref[n // local_harm, r, n % local_harm]

    def split_half(half):
        for n in orders(half, 2):
            for m in range(RADIX):
                value = jnp.concatenate(
                    [
                        jnp.concatenate([tile_of(n + i, 2 * m), tile_of(n + i, 2 * m + 1)], 1)
                        for i in range(2)
                    ],
                    0,
                )
                store_parts(part_ref, rows_of(m, n, 16), value)

    def screen_half(half):
        for n in orders(half, 1):
            points = []
            for m in range(RADIX):
                rows = rows_of(m, n, 8)
                value = (line_ref[rows, :SUB], line_ref[rows, SUB:])
                if m > 0:
                    value = twiddle_pair(
                        value, twiddle_ref[0, m : m + 1], twiddle_ref[1, m : m + 1], 1
                    )
                points.append(value)
            for k, (real, imag) in enumerate(butterflies(points, turn_pair(1))):
                lanes = slice(SUB * k, SUB * k + SUB)
                factor_real, factor_imag = screen_ref[0, n, :, lanes], screen_ref[1, n, :, lanes]
                field_ref[k, 2 * n] = real * factor_real - imag * factor_imag
                field_ref[k, 2 * n + 1] = real * factor_imag + imag * factor_real

    first, second = halves
    split_half(0)
    line_ref[first] = product(part_ref[first], inverse_ref[...])
    split_half(1)
    line_ref[second] = product(part_ref[second], inverse_ref[...])
    screen_half(0)
    screen_half(1)

    def one_block(k, carry):
        def load(index):
            return field_ref[k, index]

        def store(n, real, imag):
            if last:
                start = 128 * (n - 1) + 2 * k
                out_ref[pl.ds(start, 8, stride=16), :] = real
                out_ref[pl.ds(start + 1, 8, stride=16), :] = imag
            else:
                field_ref[k, 2 * n - 2] = real
                field_ref[k, 2 * n - 1] = imag

        couple_pixels(load, gain_ref[k], store)
        return carry

    lax.fori_loop(0, RADIX, one_block, 0)
    if last:
        return

    def spread_half(half):
        for n in orders(half, 2):
            points = [
                tuple(
                    jnp.concatenate([field_ref[k, 2 * n + c], field_ref[k, 2 * n + 2 + c]], 0)
                    for c in range(2)
                )
                for k in range(RADIX)
            ]
            forward_lanes(
                points,
                lambda m, value: store_parts(part_ref, rows_of(m, n, 16), value),
                twiddle_ref,
            )

    def store_half(half):
        result = product(part_ref[halves[half]], forward_ref[...])
        for m in range(RADIX):
            for n in orders(half, 1):
                row = height * m + 8 * (n - half * part)
                for side in range(2):
                    out_ref[n // local_harm, 2 * m + side, n % local_harm] = result[
                        row : row + 8, SUB * side : SUB * side + SUB
                    ]

    spread_half(0)
    store_half(0)
    spread_half(1)
    store_half(1)


def pixels(wavefield, screen, gain, constants, last):
    _, _, forward, inverse, twiddles = constants
    tables = [inverse, twiddles, screen, gain, forward]
    operands = in_vmem(wavefield, *tables)
    out_shape = (H * 8 * 16, SUB) if last else wavefield.shape
    return pl.pallas_call(
        functools.partial(pixel_kernel, last),
        in_specs=[IN_VMEM] * len(operands),
        out_specs=IN_VMEM,
        out_shape=pltpu.VMEM(out_shape, jnp.float32),
        scratch_shapes=[
            pltpu.VMEM((RADIX * 8 * H, 768), jnp.bfloat16),
            pltpu.VMEM((RADIX * 8 * H, 2 * SUB), jnp.float32),
            pltpu.VMEM((RADIX, 2 * H, 8, SUB), jnp.float32),
        ],
        compiler_params=pltpu.CompilerParams(vmem_limit_bytes=VMEM_LIMIT),
        cost_estimate=pl.CostEstimate(
            flops=2 * 3 * 2 * 8 * H * RADIX * 65536,
            bytes_accessed=4 * wavefield.size * 4,
            transcendentals=0,
        ),
        name="pixels_last" if last else "pixels",
    )(*operands)


def order_kernel(in_ref, out_ref, sems):
    orders = range(in_ref.shape[1])
    copies = fetch([in_ref.at[:, n] for n in orders], [out_ref.at[n] for n in orders], sems)
    for copy in copies:
        copy.wait()


def order_rows(blocks):
    groups, local_harm = blocks.shape[:2]
    return pl.pallas_call(
        order_kernel,
        in_specs=[IN_VMEM],
        out_specs=IN_HBM,
        out_shape=jax.ShapeDtypeStruct((local_harm, groups) + blocks.shape[2:], blocks.dtype),
        scratch_shapes=[pltpu.SemaphoreType.DMA((local_harm,))],
        name="order_rows",
    )(*in_vmem(blocks))


def squared_freq_at(indices, length):
    centred = jnp.where(indices < length // 2, indices, indices - length).astype(jnp.float32)
    scaled = centred * (2.0 * math.pi / length)
    return scaled * scaled


def propagator(wave_number, down_square, across_square, march_step):
    axial_square = wave_number * wave_number - down_square - across_square
    axial_root = jnp.sqrt(jnp.abs(axial_square))
    phase_turn = march_step * axial_root
    propagating = axial_square >= 0.0
    prop_real = jnp.where(propagating, jnp.cos(phase_turn), jnp.exp(-phase_turn))
    prop_imag = jnp.where(propagating, jnp.sin(phase_turn), 0.0)
    return (prop_real, prop_imag)


def propagator_tables(local_harm):
    orders = (
        lax.axis_index("harm") * local_harm + jnp.arange(local_harm, dtype=jnp.int32) + 1
    ).astype(jnp.float32)
    place = lax.axis_index("rows")
    down = RADIX * jnp.arange(SUB, dtype=jnp.int32)[None, :] + jnp.arange(
        RADIX, dtype=jnp.int32
    )[:, None]
    across = (
        RADIX * (lax.rem(place, 2) * HALF + jnp.arange(HALF, dtype=jnp.int32)) + place // 2
    )
    real, imag = propagator(
        (3.0 / H * orders)[:, None, None, None],
        squared_freq_at(down, N)[None, :, None, :],
        squared_freq_at(across, N)[None, None, :, None],
        float(DZ),
    )
    return jnp.stack([real, imag]) * (1.0 / (N * N))


def screen_tables(contrast, absorption):
    orders = jnp.arange(1, H + 1, dtype=jnp.int32).astype(jnp.float32)[:, None, None]
    damping = jnp.exp(-absorption[None] * jnp.power(orders, 1.1) * float(DZ))
    angle = 3.0 / H * orders * float(DZ) * contrast[None]
    return jnp.stack([damping * jnp.cos(angle), damping * jnp.sin(angle)])


def make_constants():
    return tuple(jnp.asarray(table) for table in lane_matrices() + (lane_twiddles(),))


def shards(pressure, contrast, absorption, nonlinearity):
    local_harm = pressure.shape[0]
    constants = make_constants()
    axes = ("harm", "rows")
    pixel_rows = 8
    row_start = lax.axis_index("harm") * pixel_rows

    def own_rows(values):
        return lax.dynamic_slice_in_dim(values, row_start, pixel_rows, 0)

    gain = own_rows(nonlinearity) * (1.0 / (H * math.sqrt(H)))
    gain = gain.reshape(pixel_rows, RADIX, SUB).transpose(1, 0, 2)
    prop = propagator_tables(local_harm)
    screen = screen_tables(own_rows(contrast), own_rows(absorption))

    lines = first_transform(pressure, constants)
    lines = lax.all_to_all(lines, "rows", 0, 0, tiled=True)
    for plane_index in range(PLANES):
        marched = march(lines, prop, (screen, gain), constants, plane_index == 0)
        shape = marched.shape
        marched = lax.all_to_all(marched.reshape((128,) + shape[2:]), axes, 0, 0, tiled=True)
        last = plane_index == PLANES - 1
        lines = pixels(marched.reshape(shape), screen, gain, constants, last)
        if not last:
            lines = lax.all_to_all(lines.reshape((128,) + shape[2:]), axes, 0, 0, tiled=True)
            lines = lines.reshape(shape)
    out = lines.reshape(8, local_harm, pixel_rows * 16, SUB)
    out = lax.all_to_all(out, "harm", 0, 0, tiled=True)
    out = order_rows(out).reshape(local_harm, 8 * pixel_rows, RADIX, 2, SUB)
    return out.transpose(0, 1, 3, 2, 4).reshape(local_harm, 8 * pixel_rows, 2, N)


def solution(mesh):
    in_specs = (P("harm", "rows", None, None), P("rows", None), P("rows", None), P("rows", None))
    out_specs = P("harm", "rows", None, None)
    return jax.shard_map(shards, mesh=mesh, in_specs=in_specs, out_specs=out_specs, check_vma=False)
```
